32 devices in a mesh: dp: 8 (over y, x, core), tensor: 4 (over z).
Axes of the slice: x: 2, y: 2, z: 4, core: 2. Of those that a mesh axis runs over, the one named last changes fastest.
Arguments:
- residual_in: bfloat16 [1024, 7168], P('dp', 'tensor'), may hold values from -6 to 6
- queries: bfloat16 [1024, 64, 192], P('dp', 'tensor'), may hold values from -41 to 41
- latent: bfloat16 [1024, 576], P('dp'), may hold values from -6 to 6
- latent_up: bfloat16 [64, 512, 256], P('tensor'), may hold values from -0.25 to 0.25
- out_proj: bfloat16 [8192, 7168], P('tensor', 'dp'), may hold values from -0.0625 to 0.0625
- norm_gain: bfloat16 [7168], P('tensor'), may hold values from 0.099609375 to 1.8984375
- expert_ids: int32 [1024, 8], P('dp'), may hold values from 0 to 255, all different within a row; in each aligned block of 128 rows (0 to 127, 128 to 255, ...) at most 8 rows name the same one
- gate_num: int32 [1024, 8], P('dp'), may hold values from 16 to 256
- slot_table: int32 [256], replicated, may hold values from 0 to 255, each once
- gate_proj: bfloat16 [8, 7168, 1024], P('dp', 'tensor'), may hold values from -0.0625 to 0.0625
- up_proj: bfloat16 [8, 7168, 1024], P('dp', 'tensor'), may hold values from -0.0625 to 0.0625
- down_proj: bfloat16 [8, 1024, 7168], P('dp', 'tensor'), may hold values from -0.1875 to 0.1875
- inv_chol: float32 [8, 1024, 128], P('dp', 'tensor'), as said below
Outputs:
- residual_out: bfloat16 [1024, 7168], P('dp', 'tensor')
- moe_out: bfloat16 [1024, 7168], P('dp', 'tensor')
- down_quant: bfloat16 [8, 1024, 7168], P('dp', 'tensor')
- panel_gram: float32 [8, 1024, 128], P('dp', 'tensor')
The draws below stay inside these ranges and needn't reach their ends.
Inputs may be any that keep to these rules, and one draw needn't show every extreme that they name: `expert_ids`: in the rows of one sequence of 128 tokens no expert is named by more than 8 rows; a row names 8 different experts. `slot_table`: each number of 0 to 255 appears once. `inv_chol`: each 128 x 128 block along the second dimension is upper triangular with a positive diagonal of at least one half.
All inputs are finite; a program needn't handle non-finite values.
Results may differ from the reference program's by a relative error of at most 0.039.
Values may be sent and summed in bfloat16 or wider, within the bound.
No kernel may reach another device: no remote copies, remote signals or barrier semaphores. Data moves between devices by JAX's collectives and lax.ppermute only.
A program may use at most 256 MiB of HBM per device.

```python
import math
import jax
import jax.numpy as jnp
import numpy as np
from jax import lax

D = 7168
FF = 1024
HEADS = 64
NOPE = 128
ROPE = 64
VHEAD = 128
LATENT = 512
EXPERTS_ALL = 256
TOPK = 8
PANEL = 128
BLK = 16
TOK_DEV = 128
KEPT = 8
CAP = 8
TOKENS = 1024
UNITS = 256
HEADS_DEV = 16
N_DP = 8
N_TENSOR = 4


def draw_queries(key, part):
    key = jax.random.fold_in(key, 11)
    shape = (TOKENS, HEADS, NOPE + ROPE)
    base = jnp.clip(jax.random.normal(jax.random.fold_in(key, 1), shape, jnp.float32), -4.0, 4.0)
    return base.astype(jnp.bfloat16)


def draw_inv_chol(key, part):
    key = jax.random.fold_in(key, 23)
    blocks = KEPT * FF // PANEL
    diagonal = jnp.exp(jax.random.uniform(jax.random.fold_in(key, 1), (blocks, PANEL), jnp.float32, math.log(0.5), math.log(1.5)))
    spread = jax.random.normal(jax.random.fold_in(key, 2), (blocks, PANEL, PANEL), jnp.float32) * (3.5 / math.sqrt(PANEL))
    upper = jnp.triu(spread, 1) + diagonal[:, :, None] * jnp.eye(PANEL, dtype=jnp.float32)[None]
    return upper.reshape(KEPT, FF, PANEL)


def set_ends(entries, key, least, top_value):
    longest = entries.shape.index(max(entries.shape))
    spots = []
    for shift in (0, 1):
        where = [jax.random.randint(jax.random.fold_in(key, axis), (), 0, length) for axis, length in enumerate(entries.shape)]
        where[longest] = (where[longest] + shift) % entries.shape[longest]
        spots.append(tuple(where))
    return entries.at[spots[0]].set(least).at[spots[1]].set(top_value)


def level_of(key, shape, cuts, least, largest):
    def one(dim, shards_of):
        heights = jax.random.uniform(jax.random.fold_in(jax.random.fold_in(key, 6), dim), (shards_of,), jnp.float32, least / len(cuts), largest / len(cuts))
        return jnp.repeat(jnp.exp(heights), shape[dim] // shards_of).reshape((-1,) + (1,) * (len(shape) - dim - 1))

    factor_of = one(*cuts[0])
    for cut in cuts[1:]:
        factor_of = factor_of * one(*cut)
    return factor_of


def routed_block(rng, own, number, rows, amount, top, most, slope):
    order = jax.random.permutation(rng, amount)
    crowded, usual = shares(amount, rows * top, most, slope, True), shares(amount, rows * top, most, slope, False)
    places = jnp.arange(amount)

    def named(tallies, rotation):
        used = int((tallies > 0).sum())
        fixed = max(1, used // 4)
        moved = fixed + (places - fixed + rotation * (used - fixed)) % max(1, amount - fixed)
        return jnp.zeros((amount,), jnp.int32).at[order[jnp.where(places < fixed, places, moved)]].set(jnp.asarray(tallies, jnp.int32))

    tallies = jnp.where(number % 4 == 0, named(crowded, number // 4), named(usual, number - number // 4 - 1))
    mixed = jax.random.permutation(jax.random.fold_in(own, 3), amount)
    donor, sink = mixed[0:amount // 2 * 2:2], mixed[1:amount // 2 * 2:2]
    slack = jnp.minimum(tallies[donor] - 1, most - tallies[sink]) // 2
    slack = jnp.where((donor == order[0]) | (sink == order[0]) | (tallies[sink] == 0), 0, jnp.maximum(slack, 0))
    moved = jax.random.randint(jax.random.fold_in(own, 4), (amount // 2,), 0, 1 << 20) % (slack + 1)
    tallies = tallies.at[donor].add(-moved).at[sink].add(moved)
    items = jnp.searchsorted(jnp.cumsum(tallies), jnp.arange(rows * top), side="right").astype(jnp.int32)
    table = items.reshape(top, rows).T
    table = table[jax.random.permutation(jax.random.fold_in(own, 1), rows)]
    rotation = jax.random.randint(jax.random.fold_in(own, 2), (rows, 1), 0, top)
    return jnp.take_along_axis(table, (jnp.arange(top)[None, :] + rotation) % top, axis=1)


def shares(number_of, total, limit, slope, full):
    loads = [(1 << 20) // math.isqrt(rank ** slope) + 1 for rank in range(1, number_of + 1)]
    largest = limit if full else min(limit, max(-(-total // number_of), total * loads[0] // sum(loads)))
    least = 1 if total - largest >= number_of - 1 else 0
    counts, rest = [largest] + [least] * (number_of - 1), total - largest - least * (number_of - 1)
    while rest > 0:
        candidates = [i for i in range(1, number_of) if counts[i] < largest] or [i for i in range(1, number_of) if counts[i] < limit]
        whole, left = sum([loads[i] for i in candidates]), rest
        for i in candidates:
            more = min(limit - counts[i], max(1, left * loads[i] // whole), rest)
            counts[i] = counts[i] + more
            rest = rest - more
    return np.array(counts)


def centred(own_key, extent, scale, limit, pieces=(), kind=jnp.bfloat16):
    loudness = level_of(own_key, extent, pieces, -0.22, 0.18) if pieces else 1.0
    entries = jax.random.normal(own_key, extent, jnp.float32) * scale * loudness
    return jnp.minimum(jnp.maximum(entries, -limit), limit).astype(kind)


def setup_inputs(seed: int = 0) -> dict:
    key_list = jax.random.split(jax.random.key(seed), 14)
    residual_in = centred(key_list[0], (TOKENS, D), 1.0, 6.0, ((0, 8), (1, 4)))
    queries = draw_queries(jax.random.fold_in(key_list[13], 71), 0)
    latent = centred(key_list[2], (TOKENS, LATENT + ROPE), 1.0, 6.0, ((0, 8),))
    latent_up = centred(key_list[3], (HEADS, LATENT, NOPE + VHEAD), LATENT ** -0.5, 0.25, ((0, 4),))
    out_proj = centred(key_list[4], (HEADS * VHEAD, D), (HEADS * VHEAD) ** -0.5, 0.0625, ((0, 4), (1, 8)))
    norm_gain = jnp.clip(1.0 + 0.18 * jax.random.normal(key_list[5], (D,), jnp.float32), 0.099609375, 1.8984375).astype(jnp.bfloat16)
    expert_ids_keys = jax.random.split(jax.random.fold_in(key_list[6], 1), TOKENS // TOK_DEV)
    expert_ids_turns = jax.random.permutation(jax.random.fold_in(key_list[6], 3), TOKENS // TOK_DEV)
    expert_ids = jax.vmap(lambda own, number: routed_block(jax.random.fold_in(key_list[6], 2), own, number, TOK_DEV, EXPERTS_ALL, TOPK, CAP, 2))(expert_ids_keys, expert_ids_turns).reshape((TOKENS, TOPK))
    gate_num = set_ends(jax.random.randint(key_list[7], (TOKENS, TOPK), 16, 257), jax.random.fold_in(key_list[7], 1), 16, 256).astype(jnp.int32)
    slot_table = jax.random.permutation(key_list[8], EXPERTS_ALL).astype(jnp.int32)
    gate_proj = centred(key_list[9], (KEPT, D, FF), D ** -0.5, 0.0625, ((0, 8), (1, 4)))
    up_proj = centred(key_list[10], (KEPT, D, FF), D ** -0.5, 0.0625, ((0, 8), (1, 4)))
    down_proj = centred(key_list[11], (KEPT, FF, D), FF ** -0.5, 0.1875, ((0, 8), (1, 4)))
    inv_chol = draw_inv_chol(jax.random.fold_in(key_list[13], 71), 0)
    return {"residual_in": residual_in, "queries": queries, "latent": latent, "latent_up": latent_up, "out_proj": out_proj, "norm_gain": norm_gain, "expert_ids": expert_ids, "gate_num": gate_num, "slot_table": slot_table, "gate_proj": gate_proj, "up_proj": up_proj, "down_proj": down_proj, "inv_chol": inv_chol}


def soft_levels(values, low, step):
    scaled = jnp.clip((values - low) / step, 0.0, 15.0)
    return low + step * (scaled - jnp.sin(2.0 * math.pi * scaled) / (2.0 * math.pi))

def quantize_panel(weight, upper):
    low = lax.optimization_barrier(jnp.min(weight, axis=0))
    high = lax.optimization_barrier(jnp.max(weight, axis=0))
    step = (high - low) / 15.0 + 1e-05
    strict = jnp.triu(upper, 1)
    diagonal = jnp.diagonal(upper)
    remaining = weight
    finished = []
    for begin in range(0, weight.shape[0], BLK):
        current = [remaining[offset] for offset in range(BLK)]
        remaining = remaining[BLK:]
        errors = []
        for offset in range(BLK):
            column = begin + offset
            levels = soft_levels(current[offset], low, step)
            finished.append(levels)
            error = (current[offset] - levels) / diagonal[column]
            errors.append(error)
            for later in range(offset + 1, BLK):
                current[later] = current[later] - strict[column, begin + later] * error
        if remaining.shape[0] > 0:
            coupling = strict[begin:begin + BLK, begin + BLK:]
            remaining = remaining - jnp.dot(coupling.T, jnp.stack(errors), precision=lax.Precision.HIGHEST)
    return jnp.stack(finished)

def reference(residual_in, queries, latent, latent_up, out_proj, norm_gain, expert_ids, gate_num, slot_table, gate_proj, up_proj, down_proj, inv_chol):
    scale = 1.0 / math.sqrt(NOPE + ROPE)
    query_seq = queries.reshape(N_DP, TOK_DEV, HEADS, NOPE + ROPE)
    latent_seq = latent.reshape(N_DP, TOK_DEV, LATENT + ROPE)
    causal = jnp.arange(TOK_DEV)[None, :] <= jnp.arange(TOK_DEV)[:, None]

    def attend(pair):
        query_blk, latent_blk = pair
        key_value = jnp.einsum('tc,hcd->thd', latent_blk[:, :LATENT].astype(jnp.float32), latent_up.astype(jnp.float32)).astype(jnp.bfloat16)
        rotary = jnp.broadcast_to(latent_blk[:, None, LATENT:], (TOK_DEV, HEADS, ROPE))
        keys = jnp.concatenate([key_value[:, :, :NOPE], rotary], axis=2)
        scores = jnp.einsum('thd,shd->hts', query_blk.astype(jnp.float32), keys.astype(jnp.float32)) * scale
        scores = jnp.where(causal[None], scores, -1e+30)
        top = lax.optimization_barrier(jnp.max(scores, axis=2, keepdims=True))
        expo = jnp.exp(scores - top)
        probs = (expo / lax.optimization_barrier(jnp.sum(expo, axis=2, keepdims=True))).astype(jnp.bfloat16)
        values = key_value[:, :, NOPE:]
        result = jnp.einsum('hts,shd->thd', probs.astype(jnp.float32), values.astype(jnp.float32)).astype(jnp.bfloat16)
        return result.reshape(TOK_DEV, HEADS * VHEAD)
    attended = lax.map(attend, (query_seq, latent_seq)).reshape(TOKENS, HEADS * VHEAD)
    group_cols = HEADS_DEV * VHEAD
    attn = jnp.zeros((TOKENS, D), jnp.float32)
    for group in range(N_TENSOR):
        piece = jnp.dot(attended[:, group * group_cols:(group + 1) * group_cols], out_proj[group * group_cols:(group + 1) * group_cols], preferred_element_type=jnp.float32)
        attn = attn + lax.optimization_barrier(piece.astype(jnp.bfloat16)).astype(jnp.float32)
    residual_out = (residual_in.astype(jnp.float32) + attn).astype(jnp.bfloat16)
    wide = residual_out.astype(jnp.float32)
    normed = (wide * lax.rsqrt(lax.optimization_barrier(jnp.mean(wide * wide, axis=1, keepdims=True)) + 1e-06) * norm_gain.astype(jnp.float32)).astype(jnp.bfloat16)
    slots = slot_table[expert_ids]
    kept = slots < KEPT
    onehot = (slots[:, :, None] == jnp.arange(KEPT, dtype=jnp.int32)[None, None, :]).astype(jnp.int32)
    onehot_seq = onehot.reshape(N_DP, TOK_DEV * TOPK, KEPT)
    before = jnp.cumsum(onehot_seq, axis=1) - onehot_seq
    position = lax.optimization_barrier(jnp.sum(before * onehot_seq, axis=2)).reshape(TOKENS, TOPK).astype(jnp.int32)
    sequence = jnp.broadcast_to((jnp.arange(TOKENS, dtype=jnp.int32) // TOK_DEV)[:, None], (TOKENS, TOPK))
    token_index = jnp.broadcast_to(jnp.arange(TOKENS, dtype=jnp.int32)[:, None], (TOKENS, TOPK))
    safe_slot = jnp.where(kept, slots, KEPT).astype(jnp.int32)
    table = jnp.full((KEPT, N_DP, CAP), TOKENS, jnp.int32)
    table = table.at[safe_slot, sequence, position].set(token_index, mode='drop')
    padded = jnp.concatenate([normed, jnp.zeros((1, D), jnp.bfloat16)], axis=0)
    slot_rows = N_DP * CAP
    panels_per = FF // PANEL

    def expert(pack):
        index_tab, gate_w, up_w, down_w, upper_w = pack
        inputs = padded[index_tab.reshape(-1)]
        gate = jnp.dot(inputs, gate_w, preferred_element_type=jnp.float32)
        upval = jnp.dot(inputs, up_w, preferred_element_type=jnp.float32)
        hidden = (jax.nn.silu(gate) * upval).astype(jnp.bfloat16)
        split = hidden.reshape(slot_rows, panels_per, PANEL).astype(jnp.float32)
        gram = (jnp.einsum('rpi,rpj->pij', split, split) / slot_rows).reshape(FF, PANEL)
        panels = down_w.astype(jnp.float32).reshape(panels_per, PANEL, D)
        uppers = upper_w.reshape(panels_per, PANEL, PANEL)
        quant = jax.vmap(quantize_panel)(panels, uppers).reshape(FF, D).astype(jnp.bfloat16)
        total = jnp.zeros((slot_rows, D), jnp.float32)
        for group in range(N_TENSOR):
            piece = jnp.dot(hidden[:, group * UNITS:(group + 1) * UNITS], quant[group * UNITS:(group + 1) * UNITS], preferred_element_type=jnp.float32)
            total = total + lax.optimization_barrier(piece.astype(jnp.bfloat16)).astype(jnp.float32)
        return (total.astype(jnp.bfloat16).reshape(N_DP, CAP, D), quant, gram)
    expert_rows, down_quant, panel_gram = lax.map(expert, (table, gate_proj, up_proj, down_proj, inv_chol))
    moe = jnp.zeros((TOKENS, D), jnp.float32)
    clipped = jnp.minimum(slots, KEPT - 1).astype(jnp.int32)
    safe_pos = jnp.minimum(position, CAP - 1).astype(jnp.int32)
    for pick in range(TOPK):
        weight = jnp.where(kept[:, pick], gate_num[:, pick].astype(jnp.float32) / 256.0, 0.0)
        values = expert_rows[clipped[:, pick], sequence[:, pick], safe_pos[:, pick]].astype(jnp.float32)
        moe = moe + weight[:, None] * values
    return (residual_out, moe.astype(jnp.bfloat16), down_quant, panel_gram)
```

```python
import math

import jax
import jax.numpy as jnp
import numpy as np
from jax import lax
from jax.experimental import pallas as pl
from jax.experimental.pallas import tpu as pltpu
from jax.sharding import PartitionSpec as P

PANEL = 128
BLK = 16
LANES = 128
SUBS = 8
CAP = 8
ROUNDER = 12582912.0
VMEM_LIMIT = 60 * 2**20


def wave_coefficients():
    nodes = 0.5 * np.cos(np.pi * (np.arange(400) + 0.5) / 800)
    values = nodes - np.sin(2 * np.pi * nodes) / (2 * np.pi)
    basis = np.stack([nodes ** (2 * power + 1) for power in range(6)], axis=1)
    return [float(c) for c in np.linalg.lstsq(basis, values, rcond=None)[0]]


WAVE = wave_coefficients()


def split_bf16(x):
    first = x.astype(jnp.bfloat16)
    rest = x - first.astype(jnp.float32)
    second = rest.astype(jnp.bfloat16)
    third = (rest - second.astype(jnp.float32)).astype(jnp.bfloat16)
    return first, second, third


def quantize_kernel(top, held, scalars, factor, source, *rest):
    done = rest[:held]
    out, weight, nat, rows, errs, levs, levels, lows, steps, scales, in_sem, out_sem, done_sem, bounce = rest[-14:]
    columns = nat.shape[1]
    groups = columns // (SUBS * LANES)
    width = groups * SUBS
    blocks = PANEL // BLK

    def fetch(c):
        lanes = pl.ds(c * SUBS * LANES, SUBS * LANES)
        return pltpu.make_async_copy(
            source.at[pl.ds(top, PANEL), lanes], weight.at[:, lanes], in_sem.at[c]
        )

    for c in range(groups):
        fetch(c).start()
    carried = [pltpu.make_async_copy(ref, bounce, done_sem) for ref in done]
    for copy in carried:
        copy.start()
    for c in range(groups):
        fetch(c).wait()
        low, high = [], []
        for s in range(SUBS):
            lanes = pl.ds((c * SUBS + s) * LANES, LANES)
            block = weight[:, lanes].astype(jnp.float32)
            nat[:, lanes] = block
            low.append(jnp.min(block, axis=0, keepdims=True))
            high.append(jnp.max(block, axis=0, keepdims=True))
        low = jnp.concatenate(low, axis=0)
        high = jnp.concatenate(high, axis=0)
        step = (high - low) / 15.0 + 1e-05
        spot = pl.ds(c * SUBS, SUBS)
        lows[spot, :] = low
        steps[spot, :] = step
        scales[spot, :] = 1.0 / step

    def block_step(b, first_row):
        base = pl.multiple_of(b * BLK, BLK)
        for g in range(width):
            rows[pl.ds(g, BLK, stride=width), :] = nat[
                pl.ds(base, BLK), g * LANES : (g + 1) * LANES
            ]
        for k in range(BLK):
            here = pl.ds(k * width, width)
            current = rows[here, :]
            for i in range(k):
                current = current - scalars[base + i, base + k] * errs[pl.ds(i * width, width), :]
            low = lows[...]
            t = jnp.clip((current - low) * scales[...], 0.0, 15.0)
            whole = (t + ROUNDER) - ROUNDER
            u = t - whole
            square = u * u
            fourth = square * square
            wave = (WAVE[0] + WAVE[1] * square) + fourth * (
                (WAVE[2] + WAVE[3] * square) + fourth * (WAVE[4] + WAVE[5] * square)
            )
            level = low + steps[...] * (whole + wave * u)
            errs[here, :] = current - level
            levs[here, :] = level
        column = lax.broadcasted_iota(jnp.int32, (BLK, PANEL), 1)
        coupling = jnp.where(column >= base + BLK, factor[pl.ds(base, BLK), :], 0.0)
        u1, u2, u3 = split_bf16(coupling)
        left = jnp.concatenate([u1, u1, u1, u2, u2, u3], axis=0)[:, first_row:]
        for c in range(groups):

            def natural(ref):
                pieces = [
                    ref[pl.ds(c * SUBS + s, BLK, stride=width), :] for s in range(SUBS)
                ]
                return jnp.concatenate(pieces, axis=1)

            span = slice(c * SUBS * LANES, (c + 1) * SUBS * LANES)
            levels[pl.ds(base, BLK), span] = natural(levs).astype(levels.dtype)
            e1, e2, e3 = split_bf16(natural(errs))
            right = jnp.concatenate([e1, e2, e3, e1, e2, e1], axis=0)
            update = lax.dot_general(
                left, right, (((0,), (0,)), ((), ())), preferred_element_type=jnp.float32
            )
            nat[first_row:, span] = nat[first_row:, span] - update

    for begin in range(0, blocks, 2):

        def body(b, carry):
            block_step(b, (begin + 1) * BLK)
            return carry

        lax.fori_loop(begin, begin + 2, body, 0)
    store = pltpu.make_async_copy(levels, out.at[pl.ds(top, PANEL), :], out_sem)
    store.start()
    for copy in carried:
        copy.wait()
        back = pltpu.make_async_copy(bounce, out.at[pl.ds(0, top), :], done_sem)
        back.start()
        back.wait()
    store.wait()


def quantize_panel(index, factor, weight, partly, *after):
    columns = weight.shape[1]
    width = columns // LANES
    wide = pltpu.VMEM((BLK * width, LANES), jnp.float32)
    small = pltpu.VMEM((width, LANES), jnp.float32)
    anywhere = pl.BlockSpec(memory_space=pl.ANY)
    return pl.pallas_call(
        lambda *refs: quantize_kernel(index * PANEL, len(partly), *refs),
        out_shape=jax.ShapeDtypeStruct(((index + 1) * PANEL, columns), jnp.bfloat16),
        in_specs=[
            pl.BlockSpec(memory_space=pltpu.SMEM),
            pl.BlockSpec(memory_space=pltpu.VMEM),
            anywhere,
        ]
        + [anywhere] * (len(partly) + len(after)),
        out_specs=anywhere,
        scratch_shapes=[
            pltpu.VMEM((PANEL, columns), jnp.bfloat16),
            pltpu.VMEM((PANEL, columns), jnp.float32),
            wide,
            wide,
            wide,
            pltpu.VMEM((PANEL, columns), jnp.bfloat16),
            small,
            small,
            small,
            pltpu.SemaphoreType.DMA((columns // (SUBS * LANES),)),
            pltpu.SemaphoreType.DMA,
            pltpu.SemaphoreType.DMA,
            pltpu.VMEM((max(1, index) * PANEL, columns), jnp.bfloat16),
        ],
        compiler_params=pltpu.CompilerParams(vmem_limit_bytes=VMEM_LIMIT),
        cost_estimate=pl.CostEstimate(
            flops=16 * 10**9, bytes_accessed=4 * PANEL * columns, transcendentals=0
        ),
    )(factor, factor, weight, *partly, *after)


def scaled_factors(upper):
    blocks = upper.reshape(-1, PANEL, PANEL)
    index = jnp.arange(PANEL)
    diagonal = jnp.sum(
        jnp.where(index[:, None] == index[None, :], blocks, 0.0), axis=2, keepdims=True
    )
    return jnp.where(index[:, None] < index[None, :], blocks / diagonal, 0.0)


def project_kernel(arrays, core, own, partner, *rest):
    rows = rest[:arrays]
    outs = rest[-arrays - 6 : -6]
    columns, left, low, high, column_sem, row_sem = rest[-6:]
    tiles = column_sem.shape[1]
    tile = columns.shape[1] // tiles
    copies = []
    for k in range(tiles):
        span = pl.ds(k * tile, tile)
        for source, turn in ((own, core[0]), (partner, 1 - core[0])):
            copies.append(
                pltpu.make_async_copy(
                    source.at[span, :],
                    columns.at[turn, span, :],
                    column_sem.at[len(copies) % 2, k],
                )
            )
    joined = len(rows[0].shape) == 3
    gathers = [
        pltpu.make_async_copy(ref, left if joined else left.at[g], row_sem.at[g])
        for g, ref in enumerate(rows)
    ]
    for copy in gathers + copies:
        copy.start()
    for copy in gathers:
        copy.wait()
    for k in range(tiles):
        copies[2 * k].wait()
        copies[2 * k + 1].wait()
        span = slice(k * tile, (k + 1) * tile)
        part = left[:, :, span].reshape(-1, tile)
        for half, total in enumerate((low, high)):
            product = jnp.dot(part, columns[half, span, :], preferred_element_type=jnp.float32)
            total[...] = product if k == 0 else total[...] + product
    count = left.shape[1]
    width = own.shape[1]
    for g in range(left.shape[0]):
        out = outs[0].at[g] if joined else outs[g]
        span = slice(g * count, (g + 1) * count)
        out[:, :width] = low[span, :].astype(jnp.bfloat16)
        out[:, width:] = high[span, :].astype(jnp.bfloat16)


def project(core, rows, own, partner, *after):
    joined = rows[0].ndim == 3
    groups = rows[0].shape[0] if joined else len(rows)
    count, depth = rows[0].shape[-2:]
    width = own.shape[1]
    shape = (groups,) * joined + (count, 2 * width)
    tiles = depth // 512
    total = groups * count
    vmem = pl.BlockSpec(memory_space=pltpu.VMEM)
    anywhere = pl.BlockSpec(memory_space=pl.ANY)
    return pl.pallas_call(
        lambda *refs: project_kernel(len(rows), *refs),
        out_shape=[jax.ShapeDtypeStruct(shape, jnp.bfloat16)] * len(rows),
        in_specs=[pl.BlockSpec(memory_space=pltpu.SMEM)]
        + [anywhere] * (2 + len(rows) + len(after)),
        out_specs=[vmem] * len(rows),
        scratch_shapes=[
            pltpu.VMEM((2, depth, width), jnp.bfloat16),
            pltpu.VMEM((groups, count, depth), jnp.bfloat16),
            pltpu.VMEM((total, width), jnp.float32),
            pltpu.VMEM((total, width), jnp.float32),
            pltpu.SemaphoreType.DMA((2, tiles)),
            pltpu.SemaphoreType.DMA((groups,)),
        ],
        compiler_params=pltpu.CompilerParams(vmem_limit_bytes=VMEM_LIMIT),
        cost_estimate=pl.CostEstimate(
            flops=4 * total * depth * width,
            bytes_accessed=2 * (total * depth + 2 * depth * width + 2 * total * width),
            transcendentals=0,
        ),
    )(core, own, partner, *rows, *after)


def front_kernel(arrived, order, residual, pick, *rest):
    front, outgoing = rest[-2:]
    ranks, per, _, width = arrived.shape
    base = jnp.dot(order[...], residual[...], preferred_element_type=jnp.float32)
    for block in range(per):
        span = slice(block * width, (block + 1) * width)
        total = sum(arrived[rank, block].astype(jnp.float32) for rank in range(ranks))
        front[:, span] = (base[:, span] + total).astype(front.dtype)
    outgoing[...] = jnp.dot(
        pick[...], front[...], preferred_element_type=jnp.float32
    ).astype(outgoing.dtype)


def make_front(arrived, order, residual, pick, *after):
    columns = residual.shape[1]
    vmem = pl.BlockSpec(memory_space=pltpu.VMEM)
    return pl.pallas_call(
        front_kernel,
        out_shape=[
            jax.ShapeDtypeStruct((order.shape[0], columns), jnp.bfloat16),
            jax.ShapeDtypeStruct((pick.shape[0], columns), jnp.bfloat16),
        ],
        in_specs=[vmem] * 4 + [pl.BlockSpec(memory_space=pl.ANY)] * len(after),
        out_specs=[vmem, vmem],
        compiler_params=pltpu.CompilerParams(vmem_limit_bytes=VMEM_LIMIT),
        cost_estimate=pl.CostEstimate(
            flops=10**8, bytes_accessed=2 * arrived.size, transcendentals=0
        ),
    )(arrived, order, residual, pick, *after)


def gate_kernel(rows, gain, gate_w, up_w, *rest):
    packed, weights, gate, up, scaled, sem = rest[-6:]
    tiles = sem.shape[1]
    tile = weights.shape[1] // tiles
    copies = []
    for k in range(tiles):
        span = pl.ds(k * tile, tile)
        for which, source in enumerate((gate_w, up_w)):
            copies.append(
                pltpu.make_async_copy(
                    source.at[span, :], weights.at[which, span, :], sem.at[which, k]
                )
            )
    for copy in copies:
        copy.start()
    wide = rows[...].astype(jnp.float32)
    squares = jnp.sum(wide * wide, axis=1, keepdims=True)
    scaled[...] = (wide * gain[...].astype(jnp.float32)).astype(jnp.bfloat16)
    for k in range(tiles):
        span = slice(k * tile, (k + 1) * tile)
        for which, total in enumerate((gate, up)):
            copies[2 * k + which].wait()
            product = jnp.dot(
                scaled[:, span], weights[which, span, :], preferred_element_type=jnp.float32
            )
            total[...] = product if k == 0 else total[...] + product
    high = squares.astype(jnp.bfloat16).astype(jnp.float32)
    lane = lax.broadcasted_iota(jnp.int32, (rows.shape[0], LANES), 1)
    tail = jnp.where(lane == 0, high, jnp.where(lane == 1, squares - high, 0.0))
    ranks, _, width = packed.shape
    units = (width - LANES) // 2
    for rank in range(ranks):
        span = slice(rank * units, (rank + 1) * units)
        packed[rank, :, :units] = gate[:, span].astype(packed.dtype)
        packed[rank, :, units : 2 * units] = up[:, span].astype(packed.dtype)
        packed[rank, :, 2 * units :] = tail.astype(packed.dtype)


def gate_and_up(rows, gain, gate_w, up_w, ranks, *after):
    count, columns = rows.shape
    hidden = gate_w.shape[1]
    tiles = 7
    shape = (ranks, count, 2 * hidden // ranks + LANES)
    vmem = pl.BlockSpec(memory_space=pltpu.VMEM)
    anywhere = pl.BlockSpec(memory_space=pl.ANY)
    return pl.pallas_call(
        gate_kernel,
        out_shape=jax.ShapeDtypeStruct(shape, jnp.bfloat16),
        in_specs=[vmem, vmem, anywhere, anywhere] + [anywhere] * len(after),
        out_specs=vmem,
        scratch_shapes=[
            pltpu.VMEM((2, columns, hidden), jnp.bfloat16),
            pltpu.VMEM((count, hidden), jnp.float32),
            pltpu.VMEM((count, hidden), jnp.float32),
            pltpu.VMEM((count, columns), jnp.bfloat16),
            pltpu.SemaphoreType.DMA((2, tiles)),
        ],
        compiler_params=pltpu.CompilerParams(vmem_limit_bytes=VMEM_LIMIT),
        cost_estimate=pl.CostEstimate(
            flops=4 * count * columns * hidden,
            bytes_accessed=4 * columns * hidden,
            transcendentals=0,
        ),
    )(rows, gain, gate_w, up_w, *after)


def expert_kernel(model_width, packed, levels, *rest):
    out, gram, held, sem = rest[-4:]
    ranks, count, width = packed.shape
    units = (width - LANES) // 2
    tiles = sem.shape[0]
    tile = held.shape[1] // tiles
    copies = []
    for k in range(tiles):
        span = pl.ds(k * tile, tile)
        copies.append(pltpu.make_async_copy(levels.at[:, span], held.at[:, span], sem.at[k]))
    for copy in copies:
        copy.start()
    summed = sum(packed[rank].astype(jnp.float32) for rank in range(ranks))
    tail = summed[:, 2 * units :]
    lane = lax.broadcasted_iota(jnp.int32, tail.shape, 1)
    squares = jnp.sum(jnp.where(lane < 2, tail, 0.0), axis=1, keepdims=True)
    inverse = lax.rsqrt(squares / model_width + 1e-06)
    gate = summed[:, :units] * inverse
    up = summed[:, units : 2 * units] * inverse
    active = (gate / (1.0 + jnp.exp(-gate)) * up).astype(jnp.bfloat16)
    for panel in range(units // PANEL):
        span = slice(panel * PANEL, (panel + 1) * PANEL)
        gram[span, :] = (
            lax.dot_general(
                active[:, span],
                active[:, span],
                (((0,), (0,)), ((), ())),
                preferred_element_type=jnp.float32,
            )
            / count
        )
    for k in range(tiles):
        span = slice(k * tile, (k + 1) * tile)
        copies[k].wait()
        out[:, span] = jnp.dot(
            active, held[:, span], preferred_element_type=jnp.float32
        ).astype(out.dtype)


def expert_outputs(packed, levels, model_width, *after):
    ranks, count, width = packed.shape
    units, columns = levels.shape
    vmem = pl.BlockSpec(memory_space=pltpu.VMEM)
    anywhere = pl.BlockSpec(memory_space=pl.ANY)
    return pl.pallas_call(
        lambda *refs: expert_kernel(model_width, *refs),
        out_shape=[
            jax.ShapeDtypeStruct((count, columns), jnp.bfloat16),
            jax.ShapeDtypeStruct((units, PANEL), jnp.float32),
        ],
        in_specs=[vmem, anywhere] + [anywhere] * len(after),
        out_specs=[vmem, vmem],
        scratch_shapes=[
            pltpu.VMEM((units, columns), jnp.bfloat16),
            pltpu.SemaphoreType.DMA((7,)),
        ],
        compiler_params=pltpu.CompilerParams(vmem_limit_bytes=VMEM_LIMIT),
        cost_estimate=pl.CostEstimate(
            flops=2 * count * units * columns,
            bytes_accessed=2 * units * columns,
            transcendentals=count * units,
        ),
    )(packed, levels, *after)


def route_kernel(owners, ids, gates, table, order, pick, combine):
    picks, tokens = ids.shape
    first = pick.shape[1]
    experts = table.shape[1]
    kept = lax.broadcasted_iota(jnp.int32, (owners, experts), 0)
    number = lax.broadcasted_iota(jnp.int32, (owners, experts), 1)
    expert_of = jnp.sum(jnp.where(table[...] == kept, number, 0), axis=1, keepdims=True)
    hit = jnp.zeros((owners, tokens), jnp.float32)
    weight = jnp.zeros((owners, tokens), jnp.float32)
    for k in range(picks):
        match = ids[k : k + 1, :] == expert_of
        hit = jnp.where(match, 1.0, hit)
        weight = jnp.where(match, gates[k : k + 1, :].astype(jnp.float32) / 256.0, weight)
    picked = jnp.max(hit, axis=0, keepdims=True)
    row = lax.broadcasted_iota(jnp.int32, (tokens, tokens), 0)
    column = lax.broadcasted_iota(jnp.int32, (tokens, tokens), 1)
    earlier = (row < column).astype(jnp.float32).astype(jnp.bfloat16)

    def before(flags):
        wide = jnp.broadcast_to(flags, (max(8, flags.shape[0]), tokens)).astype(jnp.bfloat16)
        return jnp.dot(wide, earlier, preferred_element_type=jnp.float32)[: flags.shape[0]]

    ahead = before(picked)
    token = lax.broadcasted_iota(jnp.int32, (1, tokens), 1).astype(jnp.float32)
    count = jnp.sum(picked, axis=1, keepdims=True)
    place = jnp.where(picked > 0.0, ahead, count + token - ahead).astype(jnp.int32)
    moved = (row == place).astype(jnp.float32)
    order[...] = moved.astype(jnp.bfloat16)
    position = before(hit)
    spot = lax.broadcasted_iota(jnp.int32, (CAP, tokens), 0).astype(jnp.float32)
    chosen_rows, weighted = [], []
    for s in range(owners):
        select = jnp.where(position[s : s + 1] == spot, hit[s : s + 1], 0.0)
        chosen_rows.append(select)
        weighted.append(select * weight[s : s + 1])
    combine[...] = jnp.concatenate(weighted, axis=0).astype(jnp.bfloat16)
    pick[...] = lax.dot_general(
        jnp.concatenate(chosen_rows, axis=0).astype(jnp.bfloat16),
        moved[:first].astype(jnp.bfloat16),
        (((1,), (1,)), ((), ())),
        preferred_element_type=jnp.float32,
    ).astype(jnp.bfloat16)


def route(expert_ids, gate_num, slot_table, owners, first):
    tokens = expert_ids.shape[0]
    slots = owners * CAP
    return pl.pallas_call(
        lambda *refs: route_kernel(owners, *refs),
        out_shape=[
            jax.ShapeDtypeStruct((tokens, tokens), jnp.bfloat16),
            jax.ShapeDtypeStruct((slots, first), jnp.bfloat16),
            jax.ShapeDtypeStruct((slots, tokens), jnp.bfloat16),
        ],
        cost_estimate=pl.CostEstimate(flops=10**7, bytes_accessed=10**5, transcendentals=0),
    )(expert_ids.T, gate_num.T, slot_table[None, :])


NOPE = 128
ROPE = 64
VHEAD = 128
LATENT = 512


def attend(queries, latent, latent_up):
    seq_len, head_count = queries.shape[:2]
    scale = 1.0 / math.sqrt(NOPE + ROPE)
    key_value = jnp.einsum(
        "tc,hcd->thd", latent[:, :LATENT], latent_up, preferred_element_type=jnp.float32
    ).astype(jnp.bfloat16)
    rotary = jnp.broadcast_to(latent[:, None, LATENT:], (seq_len, head_count, ROPE))
    keys = jnp.concatenate([key_value[:, :, :NOPE], rotary], axis=2)
    scores = jnp.einsum("thd,shd->hts", queries, keys, preferred_element_type=jnp.float32) * scale
    causal = jnp.arange(seq_len)[None, :] <= jnp.arange(seq_len)[:, None]
    scores = jnp.where(causal[None], scores, -1e30)
    top = jnp.max(scores, axis=2, keepdims=True)
    expo = jnp.exp(scores - top)
    probs = (expo / jnp.sum(expo, axis=2, keepdims=True)).astype(jnp.bfloat16)
    result = jnp.einsum(
        "hts,shd->thd", probs, key_value[:, :, NOPE:], preferred_element_type=jnp.float32
    )
    return result.astype(jnp.bfloat16).reshape(seq_len, head_count * VHEAD)


def chosen(onehot, rows):
    return jnp.dot(onehot, rows, preferred_element_type=jnp.float32).astype(jnp.bfloat16)


def same_cores(chips):
    return [[2 * chip + core for chip in range(chips)] for core in range(2)]


def across_chips(chunks):
    groups = same_cores(chunks.shape[0])
    return lax.all_to_all(
        chunks, "dp", split_axis=0, concat_axis=0, axis_index_groups=groups, tiled=True
    )


def to_other_chips(chunks):
    owners = 2 * len(chunks)
    moved = [chunks[0]]
    for turn in range(1, len(chunks)):
        pairs = [(place, place ^ (2 * turn)) for place in range(owners)]
        moved.append(lax.ppermute(chunks[turn], "dp", pairs))
    return moved


def to_other_ranks(chunks):
    ranks = len(chunks)
    stacked = jnp.stack(chunks)
    chip = lax.div(lax.axis_index("dp"), 2)
    rank = lax.axis_index("tensor")
    moved = []
    for shift in range(ranks):
        spot = jnp.bitwise_xor(chip, lax.rem(rank + shift, ranks))
        chunk = lax.dynamic_slice(
            stacked, (spot, 0, 0), (1,) + stacked.shape[1:], allow_negative_indices=False
        )[0]
        if shift:
            pairs = [(place, (place + shift) % ranks) for place in range(ranks)]
            chunk = lax.ppermute(chunk, "tensor", pairs)
        moved.append(chunk)
    return moved


def across_ranks(chunks, ranks):
    chips, rows, width = chunks.shape
    chunks = chunks.reshape(ranks, chips // ranks, rows, width)
    return lax.all_to_all(chunks, "tensor", split_axis=0, concat_axis=0, tiled=True)


def shards(
    residual_in,
    queries,
    latent,
    latent_up,
    out_proj,
    norm_gain,
    expert_ids,
    gate_num,
    slot_table,
    gate_proj,
    up_proj,
    down_proj,
    inv_chol,
):
    seq_len, model_cols = residual_in.shape
    owners = lax.axis_size("dp")
    ranks = lax.axis_size("tensor")

    chips = owners // 2
    first = min(seq_len, owners * CAP) if chips == ranks == 4 else seq_len
    core = lax.rem(lax.axis_index("dp"), 2)[None]
    partner = lax.ppermute(out_proj, "dp", [(i, i ^ 1) for i in range(owners)])
    order_rows, pick, combine = route(expert_ids, gate_num, slot_table, owners, first)
    factors = scaled_factors(inv_chol[0])
    weight = down_proj[0]
    panels = factors.shape[0]
    attended = attend(queries, latent, latent_up)

    copies = chosen(jnp.tile(order_rows[:first], (chips, 1)), attended)
    everyone = across_chips(copies.reshape(chips, first, -1))
    later = []
    if first < seq_len and chips == ranks:
        later = to_other_chips([chosen(order_rows[first:], attended)] * chips)
    partly = [quantize_panel(0, factors[0], weight, [], copies, *later[:1])]
    chunks = project(core, [everyone], out_proj, partner, partly[0])[0]
    arrived = across_chips(chunks)
    for panel in range(1, panels):
        partly = [quantize_panel(panel, factors[panel], weight, partly, chunks)]
    if later:
        later = project(core, later, out_proj, partner, partly[0])
    quantized = partly[0]
    front, outgoing = make_front(
        across_ranks(arrived, ranks), order_rows[:first], residual_in, pick, quantized, *later
    )
    incoming = lax.all_to_all(
        outgoing.reshape(owners, CAP, -1), "dp", split_axis=0, concat_axis=0, tiled=True
    )
    if later:
        later = to_other_chips(later)
    packed = gate_and_up(
        incoming.reshape(owners * CAP, -1),
        norm_gain[None, :],
        gate_proj[0],
        up_proj[0],
        ranks,
        *later,
    )
    packed = lax.all_to_all(packed, "tensor", split_axis=0, concat_axis=0, tiled=True)
    if later:
        later = to_other_ranks(later)
    expert_part, gram = expert_outputs(packed, quantized, model_cols * ranks, *later)
    ordered_out = front
    if later:
        ordered_in = chosen(order_rows[first:], residual_in).astype(jnp.float32)
        back = ordered_in + sum(chunk.astype(jnp.float32) for chunk in later)
        ordered_out = jnp.concatenate([front, back.astype(jnp.bfloat16)], axis=0)
    residual_out = lax.dot_general(
        order_rows, ordered_out, (((0,), (0,)), ((), ())), preferred_element_type=jnp.float32
    ).astype(jnp.bfloat16)

    parcels = (
        expert_part.reshape(owners, CAP, ranks, model_cols)
        .swapaxes(1, 2)
        .reshape(owners * ranks, CAP, model_cols)
    )
    returned = lax.all_to_all(
        parcels, ("dp", "tensor"), split_axis=0, concat_axis=0, tiled=True
    ).reshape(owners * ranks * CAP, model_cols)
    weights = jnp.broadcast_to(
        combine.reshape(owners, 1, CAP, seq_len), (owners, ranks, CAP, seq_len)
    ).reshape(owners * ranks * CAP, seq_len)
    moe = lax.dot_general(
        weights, returned, (((0,), (0,)), ((), ())), preferred_element_type=jnp.float32
    )
    return (
        residual_out,
        moe.astype(jnp.bfloat16),
        quantized[None],
        gram[None],
    )


def solution(mesh):
    placed = (
        P("dp", "tensor"),
        P("dp", "tensor", None),
        P("dp", None),
        P("tensor", None, None),
        P("tensor", "dp"),
        P("tensor"),
        P("dp", None),
        P("dp", None),
        P(),
        P("dp", "tensor", None),
        P("dp", "tensor", None),
        P("dp", "tensor", None),
        P("dp", "tensor", None),
    )
    return jax.shard_map(
        shards,
        mesh=mesh,
        in_specs=placed,
        out_specs=(
            P("dp", "tensor"),
            P("dp", "tensor"),
            P("dp", "tensor", None),
            P("dp", "tensor", None),
        ),
        check_vma=False,
    )
```

```python
import math

import jax
import jax.numpy as jnp
import numpy as np
from jax import lax
from jax.experimental import pallas as pl
from jax.experimental.pallas import tpu as pltpu
from jax.sharding import PartitionSpec as P

PANEL = 128
BLK = 16
LANES = 128
SUBS = 8
CAP = 8
ROUNDER = 12582912.0
VMEM_LIMIT = 60 * 2**20


def wave_coefficients():
    nodes = 0.5 * np.cos(np.pi * (np.arange(400) + 0.5) / 800)
    values = nodes - np.sin(2 * np.pi * nodes) / (2 * np.pi)
    basis = np.stack([nodes ** (2 * power + 1) for power in range(6)], axis=1)
    return [float(c) for c in np.linalg.lstsq(basis, values, rcond=None)[0]]


WAVE = wave_coefficients()


def split_bf16(x):
    first = x.astype(jnp.bfloat16)
    rest = x - first.astype(jnp.float32)
    second = rest.astype(jnp.bfloat16)
    third = (rest - second.astype(jnp.float32)).astype(jnp.bfloat16)
    return first, second, third


def quantize_kernel(top, held, scalars, factor, source, *rest):
    done = rest[:held]
    out, weight, nat, rows, errs, levs, levels, lows, steps, scales, in_sem, out_sem, done_sem, back_sem, bounce = rest[-15:]
    columns = nat.shape[1]
    groups = columns // (SUBS * LANES)
    width = groups * SUBS
    blocks = PANEL // BLK

    def fetch(c):
        lanes = pl.ds(c * SUBS * LANES, SUBS * LANES)
        return pltpu.make_async_copy(
            source.at[pl.ds(top, PANEL), lanes], weight.at[:, lanes], in_sem.at[c]
        )

    for c in range(groups):
        fetch(c).start()
    carried = [pltpu.make_async_copy(ref, bounce, done_sem) for ref in done]
    for copy in carried:
        copy.start()
    for c in range(groups):
        fetch(c).wait()
        low, high = [], []
        for s in range(SUBS):
            lanes = pl.ds((c * SUBS + s) * LANES, LANES)
            block = weight[:, lanes].astype(jnp.float32)
            nat[:, lanes] = block
            low.append(jnp.min(block, axis=0, keepdims=True))
            high.append(jnp.max(block, axis=0, keepdims=True))
        low = jnp.concatenate(low, axis=0)
        high = jnp.concatenate(high, axis=0)
        step = (high - low) / 15.0 + 1e-05
        spot = pl.ds(c * SUBS, SUBS)
        lows[spot, :] = low
        steps[spot, :] = step
        scales[spot, :] = 1.0 / step

    for copy in carried:
        copy.wait()
    returned = [pltpu.make_async_copy(bounce, out.at[pl.ds(0, top), :], back_sem) for _ in done]
    for copy in returned:
        copy.start()

    def finish(b):
        spot = b * BLK if isinstance(b, int) else pl.multiple_of(b * BLK, BLK)
        return pltpu.make_async_copy(
            levels.at[pl.ds(spot, BLK), :], out.at[pl.ds(top + spot, BLK), :], out_sem.at[b]
        )

    def block_step(b, first_row):
        base = b * BLK if isinstance(b, int) else pl.multiple_of(b * BLK, BLK)
        for g in range(width):
            rows[pl.ds(g, BLK, stride=width), :] = nat[
                pl.ds(base, BLK), g * LANES : (g + 1) * LANES
            ]
        for k in range(BLK):
            here = pl.ds(k * width, width)
            current = rows[here, :]
            for i in range(k):
                current = current - scalars[base + i, base + k] * errs[pl.ds(i * width, width), :]
            low = lows[...]
            t = jnp.clip((current - low) * scales[...], 0.0, 15.0)
            whole = (t + ROUNDER) - ROUNDER
            u = t - whole
            square = u * u
            fourth = square * square
            wave = (WAVE[0] + WAVE[1] * square) + fourth * (
                (WAVE[2] + WAVE[3] * square) + fourth * (WAVE[4] + WAVE[5] * square)
            )
            level = low + steps[...] * (whole + wave * u)
            errs[here, :] = current - level
            levs[here, :] = level
        column = lax.broadcasted_iota(jnp.int32, (BLK, PANEL), 1)
        coupling = jnp.where(column >= base + BLK, factor[pl.ds(base, BLK), :], 0.0)
        u1, u2, u3 = split_bf16(coupling)
        left = jnp.concatenate([u1, u1, u1, u2, u2, u3], axis=0)[:, first_row:]
        for c in range(groups):

            def natural(ref):
                pieces = [
                    ref[pl.ds(c * SUBS + s, BLK, stride=width), :] for s in range(SUBS)
                ]
                return jnp.concatenate(pieces, axis=1)

            span = slice(c * SUBS * LANES, (c + 1) * SUBS * LANES)
            levels[pl.ds(base, BLK), span] = natural(levs).astype(levels.dtype)
            if first_row == PANEL:
                continue
            e1, e2, e3 = split_bf16(natural(errs))
            right = jnp.concatenate([e1, e2, e3, e1, e2, e1], axis=0)
            update = lax.dot_general(
                left, right, (((0,), (0,)), ((), ())), preferred_element_type=jnp.float32
            )
            nat[first_row:, span] = nat[first_row:, span] - update
        finish(b).start()

    for begin in range(0, blocks - 2, 2):

        def body(b, carry):
            block_step(b, (begin + 1) * BLK)
            return carry

        lax.fori_loop(begin, begin + 2, body, 0)
    block_step(blocks - 2, (blocks - 1) * BLK)
    block_step(blocks - 1, PANEL)
    for b in range(blocks):
        finish(b).wait()
    for copy in returned:
        copy.wait()


def quantize_panel(index, factor, weight, partly, *after):
    columns = weight.shape[1]
    width = columns // LANES
    wide = pltpu.VMEM((BLK * width, LANES), jnp.float32)
    small = pltpu.VMEM((width, LANES), jnp.float32)
    anywhere = pl.BlockSpec(memory_space=pl.ANY)
    return pl.pallas_call(
        lambda *refs: quantize_kernel(index * PANEL, len(partly), *refs),
        out_shape=jax.ShapeDtypeStruct(((index + 1) * PANEL, columns), jnp.bfloat16),
        in_specs=[
            pl.BlockSpec(memory_space=pltpu.SMEM),
            pl.BlockSpec(memory_space=pltpu.VMEM),
            anywhere,
        ]
        + [anywhere] * (len(partly) + len(after)),
        out_specs=anywhere,
        scratch_shapes=[
            pltpu.VMEM((PANEL, columns), jnp.bfloat16),
            pltpu.VMEM((PANEL, columns), jnp.float32),
            wide,
            wide,
            wide,
            pltpu.VMEM((PANEL, columns), jnp.bfloat16),
            small,
            small,
            small,
            pltpu.SemaphoreType.DMA((columns // (SUBS * LANES),)),
            pltpu.SemaphoreType.DMA((PANEL // BLK,)),
            pltpu.SemaphoreType.DMA,
            pltpu.SemaphoreType.DMA,
            pltpu.VMEM((max(1, index) * PANEL, columns), jnp.bfloat16),
        ],
        compiler_params=pltpu.CompilerParams(vmem_limit_bytes=VMEM_LIMIT),
        cost_estimate=pl.CostEstimate(
            flops=16 * 10**9, bytes_accessed=4 * PANEL * columns, transcendentals=0
        ),
    )(factor, factor, weight, *partly, *after)


def scaled_factors(upper):
    blocks = upper.reshape(-1, PANEL, PANEL)
    index = jnp.arange(PANEL)
    diagonal = jnp.sum(
        jnp.where(index[:, None] == index[None, :], blocks, 0.0), axis=2, keepdims=True
    )
    return jnp.where(index[:, None] < index[None, :], blocks / diagonal, 0.0)


def project_kernel(arrays, core, own, partner, *rest):
    rows = rest[:arrays]
    outs = rest[-arrays - 6 : -6]
    columns, left, low, high, column_sem, row_sem = rest[-6:]
    tiles = column_sem.shape[1]
    tile = columns.shape[1] // tiles
    copies = []
    for k in range(tiles):
        span = pl.ds(k * tile, tile)
        for source, turn in ((own, core[0]), (partner, 1 - core[0])):
            copies.append(
                pltpu.make_async_copy(
                    source.at[span, :],
                    columns.at[turn, span, :],
                    column_sem.at[len(copies) % 2, k],
                )
            )
    joined = len(rows[0].shape) == 3
    gathers = [
        pltpu.make_async_copy(ref, left if joined else left.at[g], row_sem.at[g])
        for g, ref in enumerate(rows)
    ]
    for copy in gathers + copies:
        copy.start()
    for copy in gathers:
        copy.wait()
    for k in range(tiles):
        copies[2 * k].wait()
        copies[2 * k + 1].wait()
        span = slice(k * tile, (k + 1) * tile)
        part = left[:, :, span].reshape(-1, tile)
        for half, total in enumerate((low, high)):
            product = jnp.dot(part, columns[half, span, :], preferred_element_type=jnp.float32)
            total[...] = product if k == 0 else total[...] + product
    count = left.shape[1]
    width = own.shape[1]
    for g in range(left.shape[0]):
        out = outs[0].at[g] if joined else outs[g]
        span = slice(g * count, (g + 1) * count)
        out[:, :width] = low[span, :].astype(jnp.bfloat16)
        out[:, width:] = high[span, :].astype(jnp.bfloat16)


def project(core, rows, own, partner, *after):
    joined = rows[0].ndim == 3
    groups = rows[0].shape[0] if joined else len(rows)
    count, depth = rows[0].shape[-2:]
    width = own.shape[1]
    shape = (groups,) * joined + (count, 2 * width)
    tiles = depth // 512
    total = groups * count
    vmem = pl.BlockSpec(memory_space=pltpu.VMEM)
    anywhere = pl.BlockSpec(memory_space=pl.ANY)
    return pl.pallas_call(
        lambda *refs: project_kernel(len(rows), *refs),
        out_shape=[jax.ShapeDtypeStruct(shape, jnp.bfloat16)] * len(rows),
        in_specs=[pl.BlockSpec(memory_space=pltpu.SMEM)]
        + [anywhere] * (2 + len(rows) + len(after)),
        out_specs=[vmem] * len(rows),
        scratch_shapes=[
            pltpu.VMEM((2, depth, width), jnp.bfloat16),
            pltpu.VMEM((groups, count, depth), jnp.bfloat16),
            pltpu.VMEM((total, width), jnp.float32),
            pltpu.VMEM((total, width), jnp.float32),
            pltpu.SemaphoreType.DMA((2, tiles)),
            pltpu.SemaphoreType.DMA((groups,)),
        ],
        compiler_params=pltpu.CompilerParams(vmem_limit_bytes=VMEM_LIMIT),
        cost_estimate=pl.CostEstimate(
            flops=4 * total * depth * width,
            bytes_accessed=2 * (total * depth + 2 * depth * width + 2 * total * width),
            transcendentals=0,
        ),
    )(core, own, partner, *rows, *after)


def front_kernel(arrived, order, residual, pick, *rest):
    front, outgoing = rest[-2:]
    ranks, per, _, width = arrived.shape
    base = jnp.dot(order[...], residual[...], preferred_element_type=jnp.float32)
    for block in range(per):
        span = slice(block * width, (block + 1) * width)
        total = sum(arrived[rank, block].astype(jnp.float32) for rank in range(ranks))
        front[:, span] = (base[:, span] + total).astype(front.dtype)
    outgoing[...] = jnp.dot(
        pick[...], front[...], preferred_element_type=jnp.float32
    ).astype(outgoing.dtype)


def make_front(arrived, order, residual, pick, *after):
    columns = residual.shape[1]
    vmem = pl.BlockSpec(memory_space=pltpu.VMEM)
    return pl.pallas_call(
        front_kernel,
        out_shape=[
            jax.ShapeDtypeStruct((order.shape[0], columns), jnp.bfloat16),
            jax.ShapeDtypeStruct((pick.shape[0], columns), jnp.bfloat16),
        ],
        in_specs=[vmem] * 4 + [pl.BlockSpec(memory_space=pl.ANY)] * len(after),
        out_specs=[vmem, vmem],
        compiler_params=pltpu.CompilerParams(vmem_limit_bytes=VMEM_LIMIT),
        cost_estimate=pl.CostEstimate(
            flops=10**8, bytes_accessed=2 * arrived.size, transcendentals=0
        ),
    )(arrived, order, residual, pick, *after)


def gate_kernel(rows, gain, gate_w, up_w, *rest):
    packed, weights, gate, up, scaled, sem = rest[-6:]
    tiles = sem.shape[1]
    tile = weights.shape[1] // tiles
    copies = []
    for k in range(tiles):
        span = pl.ds(k * tile, tile)
        for which, source in enumerate((gate_w, up_w)):
            copies.append(
                pltpu.make_async_copy(
                    source.at[span, :], weights.at[which, span, :], sem.at[which, k]
                )
            )
    for copy in copies:
        copy.start()
    wide = rows[...].astype(jnp.float32)
    squares = jnp.sum(wide * wide, axis=1, keepdims=True)
    scaled[...] = (wide * gain[...].astype(jnp.float32)).astype(jnp.bfloat16)
    for k in range(tiles):
        span = slice(k * tile, (k + 1) * tile)
        for which, total in enumerate((gate, up)):
            copies[2 * k + which].wait()
            product = jnp.dot(
                scaled[:, span], weights[which, span, :], preferred_element_type=jnp.float32
            )
            total[...] = product if k == 0 else total[...] + product
    high = squares.astype(jnp.bfloat16).astype(jnp.float32)
    lane = lax.broadcasted_iota(jnp.int32, (rows.shape[0], LANES), 1)
    tail = jnp.where(lane == 0, high, jnp.where(lane == 1, squares - high, 0.0))
    ranks, _, width = packed.shape
    units = (width - LANES) // 2
    for rank in range(ranks):
        span = slice(rank * units, (rank + 1) * units)
        packed[rank, :, :units] = gate[:, span].astype(packed.dtype)
        packed[rank, :, units : 2 * units] = up[:, span].astype(packed.dtype)
        packed[rank, :, 2 * units :] = tail.astype(packed.dtype)


def gate_and_up(rows, gain, gate_w, up_w, ranks, *after):
    count, columns = rows.shape
    hidden = gate_w.shape[1]
    tiles = 7
    shape = (ranks, count, 2 * hidden // ranks + LANES)
    vmem = pl.BlockSpec(memory_space=pltpu.VMEM)
    anywhere = pl.BlockSpec(memory_space=pl.ANY)
    return pl.pallas_call(
        gate_kernel,
        out_shape=jax.ShapeDtypeStruct(shape, jnp.bfloat16),
        in_specs=[vmem, vmem, anywhere, anywhere] + [anywhere] * len(after),
        out_specs=vmem,
        scratch_shapes=[
            pltpu.VMEM((2, columns, hidden), jnp.bfloat16),
            pltpu.VMEM((count, hidden), jnp.float32),
            pltpu.VMEM((count, hidden), jnp.float32),
            pltpu.VMEM((count, columns), jnp.bfloat16),
            pltpu.SemaphoreType.DMA((2, tiles)),
        ],
        compiler_params=pltpu.CompilerParams(vmem_limit_bytes=VMEM_LIMIT),
        cost_estimate=pl.CostEstimate(
            flops=4 * count * columns * hidden,
            bytes_accessed=4 * columns * hidden,
            transcendentals=0,
        ),
    )(rows, gain, gate_w, up_w, *after)


def expert_kernel(model_width, packed, levels, *rest):
    out, gram, held, sem = rest[-4:]
    ranks, count, width = packed.shape
    units = (width - LANES) // 2
    tiles = sem.shape[0]
    tile = held.shape[1] // tiles
    copies = []
    for k in range(tiles):
        span = pl.ds(k * tile, tile)
        copies.append(pltpu.make_async_copy(levels.at[:, span], held.at[:, span], sem.at[k]))
    for copy in copies:
        copy.start()
    summed = sum(packed[rank].astype(jnp.float32) for rank in range(ranks))
    tail = summed[:, 2 * units :]
    lane = lax.broadcasted_iota(jnp.int32, tail.shape, 1)
    squares = jnp.sum(jnp.where(lane < 2, tail, 0.0), axis=1, keepdims=True)
    inverse = lax.rsqrt(squares / model_width + 1e-06)
    gate = summed[:, :units] * inverse
    up = summed[:, units : 2 * units] * inverse
    active = (gate / (1.0 + jnp.exp(-gate)) * up).astype(jnp.bfloat16)
    for panel in range(units // PANEL):
        span = slice(panel * PANEL, (panel + 1) * PANEL)
        gram[span, :] = (
            lax.dot_general(
                active[:, span],
                active[:, span],
                (((0,), (0,)), ((), ())),
                preferred_element_type=jnp.float32,
            )
            / count
        )
    for k in range(tiles):
        span = slice(k * tile, (k + 1) * tile)
        copies[k].wait()
        out[:, span] = jnp.dot(
            active, held[:, span], preferred_element_type=jnp.float32
        ).astype(out.dtype)


def expert_outputs(packed, levels, model_width, *after):
    ranks, count, width = packed.shape
    units, columns = levels.shape
    vmem = pl.BlockSpec(memory_space=pltpu.VMEM)
    anywhere = pl.BlockSpec(memory_space=pl.ANY)
    return pl.pallas_call(
        lambda *refs: expert_kernel(model_width, *refs),
        out_shape=[
            jax.ShapeDtypeStruct((count, columns), jnp.bfloat16),
            jax.ShapeDtypeStruct((units, PANEL), jnp.float32),
        ],
        in_specs=[vmem, anywhere] + [anywhere] * len(after),
        out_specs=[vmem, vmem],
        scratch_shapes=[
            pltpu.VMEM((units, columns), jnp.bfloat16),
            pltpu.SemaphoreType.DMA((7,)),
        ],
        compiler_params=pltpu.CompilerParams(vmem_limit_bytes=VMEM_LIMIT),
        cost_estimate=pl.CostEstimate(
            flops=2 * count * units * columns,
            bytes_accessed=2 * units * columns,
            transcendentals=count * units,
        ),
    )(packed, levels, *after)


def route_kernel(owners, ids, gates, table, order, pick, combine, front, copies):
    picks, tokens = ids.shape
    first = pick.shape[1]
    experts = table.shape[1]
    kept = lax.broadcasted_iota(jnp.int32, (owners, experts), 0)
    number = lax.broadcasted_iota(jnp.int32, (owners, experts), 1)
    expert_of = jnp.sum(jnp.where(table[...] == kept, number, 0), axis=1, keepdims=True)
    hit = jnp.zeros((owners, tokens), jnp.float32)
    weight = jnp.zeros((owners, tokens), jnp.float32)
    for k in range(picks):
        match = ids[k : k + 1, :] == expert_of
        hit = jnp.where(match, 1.0, hit)
        weight = jnp.where(match, gates[k : k + 1, :].astype(jnp.float32) / 256.0, weight)
    picked = jnp.max(hit, axis=0, keepdims=True)
    row = lax.broadcasted_iota(jnp.int32, (tokens, tokens), 0)
    column = lax.broadcasted_iota(jnp.int32, (tokens, tokens), 1)
    earlier = (row < column).astype(jnp.float32).astype(jnp.bfloat16)

    def before(flags):
        wide = jnp.broadcast_to(flags, (max(8, flags.shape[0]), tokens)).astype(jnp.bfloat16)
        return jnp.dot(wide, earlier, preferred_element_type=jnp.float32)[: flags.shape[0]]

    ahead = before(picked)
    token = lax.broadcasted_iota(jnp.int32, (1, tokens), 1).astype(jnp.float32)
    count = jnp.sum(picked, axis=1, keepdims=True)
    place = jnp.where(picked > 0.0, ahead, count + token - ahead).astype(jnp.int32)
    moved = (row == place).astype(jnp.float32)
    order[...] = moved.astype(jnp.bfloat16)
    front[...] = moved[:first].astype(jnp.bfloat16)
    for chip in range(copies.shape[0] // first):
        copies[chip * first : (chip + 1) * first, :] = moved[:first].astype(jnp.bfloat16)
    position = before(hit)
    spot = lax.broadcasted_iota(jnp.int32, (CAP, tokens), 0).astype(jnp.float32)
    chosen_rows, weighted = [], []
    for s in range(owners):
        select = jnp.where(position[s : s + 1] == spot, hit[s : s + 1], 0.0)
        chosen_rows.append(select)
        weighted.append(select * weight[s : s + 1])
    combine[...] = jnp.concatenate(weighted, axis=0).astype(jnp.bfloat16)
    pick[...] = lax.dot_general(
        jnp.concatenate(chosen_rows, axis=0).astype(jnp.bfloat16),
        moved[:first].astype(jnp.bfloat16),
        (((1,), (1,)), ((), ())),
        preferred_element_type=jnp.float32,
    ).astype(jnp.bfloat16)


def route(expert_ids, gate_num, slot_table, owners, first):
    tokens = expert_ids.shape[0]
    slots = owners * CAP
    return pl.pallas_call(
        lambda *refs: route_kernel(owners, *refs),
        out_shape=[
            jax.ShapeDtypeStruct((tokens, tokens), jnp.bfloat16),
            jax.ShapeDtypeStruct((slots, first), jnp.bfloat16),
            jax.ShapeDtypeStruct((slots, tokens), jnp.bfloat16),
            jax.ShapeDtypeStruct((first, tokens), jnp.bfloat16),
            jax.ShapeDtypeStruct((owners // 2 * first, tokens), jnp.bfloat16),
        ],
        cost_estimate=pl.CostEstimate(flops=10**7, bytes_accessed=10**5, transcendentals=0),
    )(expert_ids.T, gate_num.T, slot_table[None, :])


NOPE = 128
ROPE = 64
VHEAD = 128
LATENT = 512


def attend(queries, latent, latent_up):
    seq_len, head_count = queries.shape[:2]
    scale = 1.0 / math.sqrt(NOPE + ROPE)
    key_value = jnp.einsum(
        "tc,hcd->thd", latent[:, :LATENT], latent_up, preferred_element_type=jnp.float32
    ).astype(jnp.bfloat16)
    rotary = jnp.broadcast_to(latent[:, None, LATENT:], (seq_len, head_count, ROPE))
    keys = jnp.concatenate([key_value[:, :, :NOPE], rotary], axis=2)
    scores = jnp.einsum("thd,shd->hts", queries, keys, preferred_element_type=jnp.float32) * scale
    causal = jnp.arange(seq_len)[None, :] <= jnp.arange(seq_len)[:, None]
    scores = jnp.where(causal[None], scores, -1e30)
    top = jnp.max(scores, axis=2, keepdims=True)
    expo = jnp.exp(scores - top)
    probs = (expo / jnp.sum(expo, axis=2, keepdims=True)).astype(jnp.bfloat16)
    result = jnp.einsum(
        "hts,shd->thd", probs, key_value[:, :, NOPE:], preferred_element_type=jnp.float32
    )
    return result.astype(jnp.bfloat16).reshape(seq_len, head_count * VHEAD)


def chosen(onehot, rows):
    return jnp.dot(onehot, rows, preferred_element_type=jnp.float32).astype(jnp.bfloat16)


def same_cores(chips):
    return [[2 * chip + core for chip in range(chips)] for core in range(2)]


def across_chips(chunks):
    groups = same_cores(chunks.shape[0])
    return lax.all_to_all(
        chunks, "dp", split_axis=0, concat_axis=0, axis_index_groups=groups, tiled=True
    )


def to_other_chips(chunks):
    owners = 2 * len(chunks)
    moved = [chunks[0]]
    for turn in range(1, len(chunks)):
        pairs = [(place, place ^ (2 * turn)) for place in range(owners)]
        moved.append(lax.ppermute(chunks[turn], "dp", pairs))
    return moved


def in_order_of_ranks(chunks):
    ranks = len(chunks)
    stacked = jnp.stack(chunks)
    chip = lax.div(lax.axis_index("dp"), 2)
    rank = lax.axis_index("tensor")
    ordered = []
    for shift in range(ranks):
        spot = jnp.bitwise_xor(chip, lax.rem(rank + shift, ranks))
        chunk = lax.dynamic_slice(
            stacked, (spot, 0, 0), (1,) + stacked.shape[1:], allow_negative_indices=False
        )
        ordered.append(chunk[0])
    return ordered


def to_other_ranks(chunks):
    ranks = len(chunks)
    moved = [chunks[0]]
    for shift in range(1, ranks):
        pairs = [(place, (place + shift) % ranks) for place in range(ranks)]
        moved.append(lax.ppermute(chunks[shift], "tensor", pairs))
    return moved


def across_ranks(chunks, ranks):
    chips, rows, width = chunks.shape
    chunks = chunks.reshape(ranks, chips // ranks, rows, width)
    return lax.all_to_all(chunks, "tensor", split_axis=0, concat_axis=0, tiled=True)


def shards(
    residual_in,
    queries,
    latent,
    latent_up,
    out_proj,
    norm_gain,
    expert_ids,
    gate_num,
    slot_table,
    gate_proj,
    up_proj,
    down_proj,
    inv_chol,
):
    seq_len, model_cols = residual_in.shape
    owners = lax.axis_size("dp")
    ranks = lax.axis_size("tensor")

    chips = owners // 2
    first = min(seq_len, owners * CAP) if chips == ranks == 4 else seq_len
    core = lax.rem(lax.axis_index("dp"), 2)[None]
    partner = lax.ppermute(out_proj, "dp", [(i, i ^ 1) for i in range(owners)])
    order_rows, pick, combine, order_first, order_copies = route(
        expert_ids, gate_num, slot_table, owners, first
    )
    factors = scaled_factors(inv_chol[0])
    weight = down_proj[0]
    panels = factors.shape[0]
    attended = attend(queries, latent, latent_up)

    copies = chosen(order_copies, attended)
    everyone = across_chips(copies.reshape(chips, first, -1))
    later = []
    if first < seq_len and chips == ranks:
        later = to_other_chips([chosen(order_rows[first:], attended)] * chips)
    partly = [quantize_panel(0, factors[0], weight, [], copies, *later[:1])]
    chunks = project(core, [everyone], out_proj, partner, partly[0])[0]
    arrived = across_chips(chunks)
    for panel in range(1, panels):
        partly = [quantize_panel(panel, factors[panel], weight, partly, chunks)]
    if later:
        later = project(core, later, out_proj, partner, partly[0])
    quantized = partly[0]
    front, outgoing = make_front(
        across_ranks(arrived, ranks), order_first, residual_in, pick, quantized
    )
    incoming = lax.all_to_all(
        outgoing.reshape(owners, CAP, -1), "dp", split_axis=0, concat_axis=0, tiled=True
    )
    packed = gate_and_up(
        incoming.reshape(owners * CAP, -1),
        norm_gain[None, :],
        gate_proj[0],
        up_proj[0],
        ranks,
        *later,
    )
    packed = lax.all_to_all(packed, "tensor", split_axis=0, concat_axis=0, tiled=True)
    if later:
        later = in_order_of_ranks(to_other_chips(later))
    expert_part, gram = expert_outputs(packed, quantized, model_cols * ranks, *later)
    if later:
        later = to_other_ranks(later)
    ordered_out = front
    if later:
        ordered_in = chosen(order_rows[first:], residual_in).astype(jnp.float32)
        back = ordered_in + sum(chunk.astype(jnp.float32) for chunk in later)
        ordered_out = jnp.concatenate([front, back.astype(jnp.bfloat16)], axis=0)
    residual_out = lax.dot_general(
        order_rows, ordered_out, (((0,), (0,)), ((), ())), preferred_element_type=jnp.float32
    ).astype(jnp.bfloat16)

    parcels = (
        expert_part.reshape(owners, CAP, ranks, model_cols)
        .swapaxes(1, 2)
        .reshape(owners * ranks, CAP, model_cols)
    )
    returned = lax.all_to_all(
        parcels, ("dp", "tensor"), split_axis=0, concat_axis=0, tiled=True
    ).reshape(owners * ranks * CAP, model_cols)
    weights = jnp.broadcast_to(
        combine.reshape(owners, 1, CAP, seq_len), (owners, ranks, CAP, seq_len)
    ).reshape(owners * ranks * CAP, seq_len)
    moe = lax.dot_general(
        weights, returned, (((0,), (0,)), ((), ())), preferred_element_type=jnp.float32
    )
    return (
        residual_out,
        moe.astype(jnp.bfloat16),
        quantized[None],
        gram[None],
    )


def solution(mesh):
    placed = (
        P("dp", "tensor"),
        P("dp", "tensor", None),
        P("dp", None),
        P("tensor", None, None),
        P("tensor", "dp"),
        P("tensor"),
        P("dp", None),
        P("dp", None),
        P(),
        P("dp", "tensor", None),
        P("dp", "tensor", None),
        P("dp", "tensor", None),
        P("dp", "tensor", None),
    )
    return jax.shard_map(
        shards,
        mesh=mesh,
        in_specs=placed,
        out_specs=(
            P("dp", "tensor"),
            P("dp", "tensor"),
            P("dp", "tensor", None),
            P("dp", "tensor", None),
        ),
        check_vma=False,
    )
```

```python
import math

import jax
import jax.numpy as jnp
import numpy as np
from jax import lax
from jax.experimental import pallas as pl
from jax.experimental.pallas import tpu as pltpu
from jax.sharding import PartitionSpec as P

PANEL = 128
BLK = 16
LANES = 128
SUBS = 8
CAP = 8
ROUNDER = 12582912.0
VMEM_LIMIT = 60 * 2**20


def wave_coefficients():
    nodes = 0.5 * np.cos(np.pi * (np.arange(400) + 0.5) / 800)
    values = nodes - np.sin(2 * np.pi * nodes) / (2 * np.pi)
    basis = np.stack([nodes ** (2 * power + 1) for power in range(6)], axis=1)
    return [float(c) for c in np.linalg.lstsq(basis, values, rcond=None)[0]]


WAVE = wave_coefficients()


def split_bf16(x):
    first = x.astype(jnp.bfloat16)
    rest = x - first.astype(jnp.float32)
    second = rest.astype(jnp.bfloat16)
    third = (rest - second.astype(jnp.float32)).astype(jnp.bfloat16)
    return first, second, third


def quantize_kernel(top, held, scalars, factor, source, *rest):
    done = rest[:held]
    out, weight, nat, rows, errs, levs, levels, lows, steps, scales, in_sem, out_sem, done_sem, back_sem, bounce = rest[-15:]
    columns = nat.shape[1]
    groups = columns // (SUBS * LANES)
    width = groups * SUBS
    blocks = PANEL // BLK

    def fetch(c):
        lanes = pl.ds(c * SUBS * LANES, SUBS * LANES)
        return pltpu.make_async_copy(
            source.at[pl.ds(top, PANEL), lanes], weight.at[:, lanes], in_sem.at[c]
        )

    for c in range(groups):
        fetch(c).start()
    carried = [pltpu.make_async_copy(ref, bounce, done_sem) for ref in done]
    for copy in carried:
        copy.start()
    for c in range(groups):
        fetch(c).wait()
        low, high = [], []
        for s in range(SUBS):
            lanes = pl.ds((c * SUBS + s) * LANES, LANES)
            block = weight[:, lanes].astype(jnp.float32)
            nat[:, lanes] = block
            low.append(jnp.min(block, axis=0, keepdims=True))
            high.append(jnp.max(block, axis=0, keepdims=True))
        low = jnp.concatenate(low, axis=0)
        high = jnp.concatenate(high, axis=0)
        step = (high - low) / 15.0 + 1e-05
        spot = pl.ds(c * SUBS, SUBS)
        lows[spot, :] = low
        steps[spot, :] = step
        scales[spot, :] = 1.0 / step

    for copy in carried:
        copy.wait()
    returned = [pltpu.make_async_copy(bounce, out.at[pl.ds(0, top), :], back_sem) for _ in done]
    for copy in returned:
        copy.start()

    def finish(b):
        spot = b * BLK if isinstance(b, int) else pl.multiple_of(b * BLK, BLK)
        return pltpu.make_async_copy(
            levels.at[pl.ds(spot, BLK), :], out.at[pl.ds(top + spot, BLK), :], out_sem.at[b]
        )

    def block_step(b, first_row):
        base = b * BLK if isinstance(b, int) else pl.multiple_of(b * BLK, BLK)
        for g in range(width):
            rows[pl.ds(g, BLK, stride=width), :] = nat[
                pl.ds(base, BLK), g * LANES : (g + 1) * LANES
            ]
        for k in range(BLK):
            here = pl.ds(k * width, width)
            current = rows[here, :]
            for i in range(k):
                current = current - scalars[base + i, base + k] * errs[pl.ds(i * width, width), :]
            low = lows[...]
            t = jnp.clip((current - low) * scales[...], 0.0, 15.0)
            whole = (t + ROUNDER) - ROUNDER
            u = t - whole
            square = u * u
            fourth = square * square
            wave = (WAVE[0] + WAVE[1] * square) + fourth * (
                (WAVE[2] + WAVE[3] * square) + fourth * (WAVE[4] + WAVE[5] * square)
            )
            level = low + steps[...] * (whole + wave * u)
            errs[here, :] = current - level
            levs[here, :] = level
        column = lax.broadcasted_iota(jnp.int32, (BLK, PANEL), 1)
        coupling = jnp.where(column >= base + BLK, factor[pl.ds(base, BLK), :], 0.0)
        u1, u2, u3 = split_bf16(coupling)
        left = jnp.concatenate([u1, u1, u1, u2, u2, u3], axis=0)[:, first_row:]
        for c in range(groups):

            def natural(ref):
                pieces = [
                    ref[pl.ds(c * SUBS + s, BLK, stride=width), :] for s in range(SUBS)
                ]
                return jnp.concatenate(pieces, axis=1)

            span = slice(c * SUBS * LANES, (c + 1) * SUBS * LANES)
            levels[pl.ds(base, BLK), span] = natural(levs).astype(levels.dtype)
            if first_row == PANEL:
                continue
            e1, e2, e3 = split_bf16(natural(errs))
            right = jnp.concatenate([e1, e2, e3, e1, e2, e1], axis=0)
            update = lax.dot_general(
                left, right, (((0,), (0,)), ((), ())), preferred_element_type=jnp.float32
            )
            nat[first_row:, span] = nat[first_row:, span] - update
        finish(b).start()

    for begin in range(0, blocks - 2, 2):

        def body(b, carry):
            block_step(b, (begin + 1) * BLK)
            return carry

        lax.fori_loop(begin, begin + 2, body, 0)
    block_step(blocks - 2, (blocks - 1) * BLK)
    block_step(blocks - 1, PANEL)
    for b in range(blocks):
        finish(b).wait()
    for copy in returned:
        copy.wait()


def quantize_panel(index, factor, weight, partly, *after):
    columns = weight.shape[1]
    width = columns // LANES
    wide = pltpu.VMEM((BLK * width, LANES), jnp.float32)
    small = pltpu.VMEM((width, LANES), jnp.float32)
    anywhere = pl.BlockSpec(memory_space=pl.ANY)
    return pl.pallas_call(
        lambda *refs: quantize_kernel(index * PANEL, len(partly), *refs),
        out_shape=jax.ShapeDtypeStruct(((index + 1) * PANEL, columns), jnp.bfloat16),
        in_specs=[
            pl.BlockSpec(memory_space=pltpu.SMEM),
            pl.BlockSpec(memory_space=pltpu.VMEM),
            anywhere,
        ]
        + [anywhere] * (len(partly) + len(after)),
        out_specs=anywhere,
        scratch_shapes=[
            pltpu.VMEM((PANEL, columns), jnp.bfloat16),
            pltpu.VMEM((PANEL, columns), jnp.float32),
            wide,
            wide,
            wide,
            pltpu.VMEM((PANEL, columns), jnp.bfloat16),
            small,
            small,
            small,
            pltpu.SemaphoreType.DMA((columns // (SUBS * LANES),)),
            pltpu.SemaphoreType.DMA((PANEL // BLK,)),
            pltpu.SemaphoreType.DMA,
            pltpu.SemaphoreType.DMA,
            pltpu.VMEM((max(1, index) * PANEL, columns), jnp.bfloat16),
        ],
        compiler_params=pltpu.CompilerParams(vmem_limit_bytes=VMEM_LIMIT),
        cost_estimate=pl.CostEstimate(
            flops=16 * 10**9, bytes_accessed=4 * PANEL * columns, transcendentals=0
        ),
    )(factor, factor, weight, *partly, *after)


def scaled_factors(upper):
    blocks = upper.reshape(-1, PANEL, PANEL)
    index = jnp.arange(PANEL)
    diagonal = jnp.sum(
        jnp.where(index[:, None] == index[None, :], blocks, 0.0), axis=2, keepdims=True
    )
    return jnp.where(index[:, None] < index[None, :], blocks / diagonal, 0.0)


def project_kernel(arrays, core, own, partner, *rest):
    rows = rest[:arrays]
    outs = rest[-arrays - 6 : -6]
    columns, left, low, high, column_sem, row_sem = rest[-6:]
    tiles = column_sem.shape[1]
    tile = columns.shape[1] // tiles
    copies = []
    for k in range(tiles):
        span = pl.ds(k * tile, tile)
        for source, turn in ((own, core[0]), (partner, 1 - core[0])):
            copies.append(
                pltpu.make_async_copy(
                    source.at[span, :],
                    columns.at[turn, span, :],
                    column_sem.at[len(copies) % 2, k],
                )
            )
    joined = len(rows[0].shape) == 3
    gathers = [
        pltpu.make_async_copy(ref, left if joined else left.at[g], row_sem.at[g])
        for g, ref in enumerate(rows)
    ]
    for copy in gathers + copies:
        copy.start()
    for copy in gathers:
        copy.wait()
    for k in range(tiles):
        copies[2 * k].wait()
        copies[2 * k + 1].wait()
        span = slice(k * tile, (k + 1) * tile)
        part = left[:, :, span].reshape(-1, tile)
        for half, total in enumerate((low, high)):
            product = jnp.dot(part, columns[half, span, :], preferred_element_type=jnp.float32)
            total[...] = product if k == 0 else total[...] + product
    count = left.shape[1]
    width = own.shape[1]
    for g in range(left.shape[0]):
        out = outs[0].at[g] if joined else outs[g]
        span = slice(g * count, (g + 1) * count)
        out[:, :width] = low[span, :].astype(jnp.bfloat16)
        out[:, width:] = high[span, :].astype(jnp.bfloat16)


def project(core, rows, own, partner, *after):
    joined = rows[0].ndim == 3
    groups = rows[0].shape[0] if joined else len(rows)
    count, depth = rows[0].shape[-2:]
    width = own.shape[1]
    shape = (groups,) * joined + (count, 2 * width)
    tiles = depth // 512
    total = groups * count
    vmem = pl.BlockSpec(memory_space=pltpu.VMEM)
    anywhere = pl.BlockSpec(memory_space=pl.ANY)
    return pl.pallas_call(
        lambda *refs: project_kernel(len(rows), *refs),
        out_shape=[jax.ShapeDtypeStruct(shape, jnp.bfloat16)] * len(rows),
        in_specs=[pl.BlockSpec(memory_space=pltpu.SMEM)]
        + [anywhere] * (2 + len(rows) + len(after)),
        out_specs=[vmem] * len(rows),
        scratch_shapes=[
            pltpu.VMEM((2, depth, width), jnp.bfloat16),
            pltpu.VMEM((groups, count, depth), jnp.bfloat16),
            pltpu.VMEM((total, width), jnp.float32),
            pltpu.VMEM((total, width), jnp.float32),
            pltpu.SemaphoreType.DMA((2, tiles)),
            pltpu.SemaphoreType.DMA((groups,)),
        ],
        compiler_params=pltpu.CompilerParams(vmem_limit_bytes=VMEM_LIMIT),
        cost_estimate=pl.CostEstimate(
            flops=4 * total * depth * width,
            bytes_accessed=2 * (total * depth + 2 * depth * width + 2 * total * width),
            transcendentals=0,
        ),
    )(core, own, partner, *rows, *after)


def front_kernel(arrived, order, residual, pick, *rest):
    front, outgoing = rest[-2:]
    ranks, per, _, width = arrived.shape
    base = jnp.dot(order[...], residual[...], preferred_element_type=jnp.float32)
    for block in range(per):
        span = slice(block * width, (block + 1) * width)
        total = sum(arrived[rank, block].astype(jnp.float32) for rank in range(ranks))
        front[:, span] = (base[:, span] + total).astype(front.dtype)
    outgoing[...] = jnp.dot(
        pick[...], front[...], preferred_element_type=jnp.float32
    ).astype(outgoing.dtype)


def make_front(arrived, order, residual, pick, *after):
    columns = residual.shape[1]
    vmem = pl.BlockSpec(memory_space=pltpu.VMEM)
    return pl.pallas_call(
        front_kernel,
        out_shape=[
            jax.ShapeDtypeStruct((order.shape[0], columns), jnp.bfloat16),
            jax.ShapeDtypeStruct((pick.shape[0], columns), jnp.bfloat16),
        ],
        in_specs=[vmem] * 4 + [pl.BlockSpec(memory_space=pl.ANY)] * len(after),
        out_specs=[vmem, vmem],
        compiler_params=pltpu.CompilerParams(vmem_limit_bytes=VMEM_LIMIT),
        cost_estimate=pl.CostEstimate(
            flops=10**8, bytes_accessed=2 * arrived.size, transcendentals=0
        ),
    )(arrived, order, residual, pick, *after)


def arrange_kernel(count, spots, *rest):
    chunks, outs = rest[:count], rest[-count:]
    for place, out in enumerate(outs):
        for number, chunk in enumerate(chunks):

            @pl.when(spots[place] == number)
            def _():
                out[...] = chunk[...]


def arrange(spots, chunks, *after):
    vmem = pl.BlockSpec(memory_space=pltpu.VMEM)
    return pl.pallas_call(
        lambda *refs: arrange_kernel(len(chunks), *refs),
        out_shape=[jax.ShapeDtypeStruct(chunk.shape, chunk.dtype) for chunk in chunks],
        in_specs=[pl.BlockSpec(memory_space=pltpu.SMEM)]
        + [vmem] * len(chunks)
        + [pl.BlockSpec(memory_space=pl.ANY)] * len(after),
        out_specs=[vmem] * len(chunks),
        compiler_params=pltpu.CompilerParams(vmem_limit_bytes=VMEM_LIMIT),
        cost_estimate=pl.CostEstimate(
            flops=0, bytes_accessed=4 * len(chunks) * chunks[0].size, transcendentals=0
        ),
    )(spots, *chunks, *after)


def gate_kernel(rows, gain, gate_w, up_w, *rest):
    packed, weights, gate, up, scaled, sem = rest[-6:]
    tiles = sem.shape[1]
    tile = weights.shape[1] // tiles
    copies = []
    for k in range(tiles):
        span = pl.ds(k * tile, tile)
        for which, source in enumerate((gate_w, up_w)):
            copies.append(
                pltpu.make_async_copy(
                    source.at[span, :], weights.at[which, span, :], sem.at[which, k]
                )
            )
    for copy in copies:
        copy.start()
    wide = rows[...].astype(jnp.float32)
    squares = jnp.sum(wide * wide, axis=1, keepdims=True)
    scaled[...] = (wide * gain[...].astype(jnp.float32)).astype(jnp.bfloat16)
    for k in range(tiles):
        span = slice(k * tile, (k + 1) * tile)
        for which, total in enumerate((gate, up)):
            copies[2 * k + which].wait()
            product = jnp.dot(
                scaled[:, span], weights[which, span, :], preferred_element_type=jnp.float32
            )
            total[...] = product if k == 0 else total[...] + product
    high = squares.astype(jnp.bfloat16).astype(jnp.float32)
    lane = lax.broadcasted_iota(jnp.int32, (rows.shape[0], LANES), 1)
    tail = jnp.where(lane == 0, high, jnp.where(lane == 1, squares - high, 0.0))
    ranks, _, width = packed.shape
    units = (width - LANES) // 2
    for rank in range(ranks):
        span = slice(rank * units, (rank + 1) * units)
        packed[rank, :, :units] = gate[:, span].astype(packed.dtype)
        packed[rank, :, units : 2 * units] = up[:, span].astype(packed.dtype)
        packed[rank, :, 2 * units :] = tail.astype(packed.dtype)


def gate_and_up(rows, gain, gate_w, up_w, ranks, *after):
    count, columns = rows.shape
    hidden = gate_w.shape[1]
    tiles = 7
    shape = (ranks, count, 2 * hidden // ranks + LANES)
    vmem = pl.BlockSpec(memory_space=pltpu.VMEM)
    anywhere = pl.BlockSpec(memory_space=pl.ANY)
    return pl.pallas_call(
        gate_kernel,
        out_shape=jax.ShapeDtypeStruct(shape, jnp.bfloat16),
        in_specs=[vmem, vmem, anywhere, anywhere] + [anywhere] * len(after),
        out_specs=vmem,
        scratch_shapes=[
            pltpu.VMEM((2, columns, hidden), jnp.bfloat16),
            pltpu.VMEM((count, hidden), jnp.float32),
            pltpu.VMEM((count, hidden), jnp.float32),
            pltpu.VMEM((count, columns), jnp.bfloat16),
            pltpu.SemaphoreType.DMA((2, tiles)),
        ],
        compiler_params=pltpu.CompilerParams(vmem_limit_bytes=VMEM_LIMIT),
        cost_estimate=pl.CostEstimate(
            flops=4 * count * columns * hidden,
            bytes_accessed=4 * columns * hidden,
            transcendentals=0,
        ),
    )(rows, gain, gate_w, up_w, *after)


def expert_kernel(model_width, packed, levels, *rest):
    out, gram, held, sem = rest[-4:]
    ranks, count, width = packed.shape
    units = (width - LANES) // 2
    tiles = sem.shape[0]
    tile = held.shape[1] // tiles
    copies = []
    for k in range(tiles):
        span = pl.ds(k * tile, tile)
        copies.append(pltpu.make_async_copy(levels.at[:, span], held.at[:, span], sem.at[k]))
    for copy in copies:
        copy.start()
    summed = sum(packed[rank].astype(jnp.float32) for rank in range(ranks))
    tail = summed[:, 2 * units :]
    lane = lax.broadcasted_iota(jnp.int32, tail.shape, 1)
    squares = jnp.sum(jnp.where(lane < 2, tail, 0.0), axis=1, keepdims=True)
    inverse = lax.rsqrt(squares / model_width + 1e-06)
    gate = summed[:, :units] * inverse
    up = summed[:, units : 2 * units] * inverse
    active = (gate / (1.0 + jnp.exp(-gate)) * up).astype(jnp.bfloat16)
    for panel in range(units // PANEL):
        span = slice(panel * PANEL, (panel + 1) * PANEL)
        gram[span, :] = (
            lax.dot_general(
                active[:, span],
                active[:, span],
                (((0,), (0,)), ((), ())),
                preferred_element_type=jnp.float32,
            )
            / count
        )
    for k in range(tiles):
        span = slice(k * tile, (k + 1) * tile)
        copies[k].wait()
        out[:, span] = jnp.dot(
            active, held[:, span], preferred_element_type=jnp.float32
        ).astype(out.dtype)


def expert_outputs(packed, levels, model_width, *after):
    ranks, count, width = packed.shape
    units, columns = levels.shape
    vmem = pl.BlockSpec(memory_space=pltpu.VMEM)
    anywhere = pl.BlockSpec(memory_space=pl.ANY)
    return pl.pallas_call(
        lambda *refs: expert_kernel(model_width, *refs),
        out_shape=[
            jax.ShapeDtypeStruct((count, columns), jnp.bfloat16),
            jax.ShapeDtypeStruct((units, PANEL), jnp.float32),
        ],
        in_specs=[vmem, anywhere] + [anywhere] * len(after),
        out_specs=[vmem, vmem],
        scratch_shapes=[
            pltpu.VMEM((units, columns), jnp.bfloat16),
            pltpu.SemaphoreType.DMA((7,)),
        ],
        compiler_params=pltpu.CompilerParams(vmem_limit_bytes=VMEM_LIMIT),
        cost_estimate=pl.CostEstimate(
            flops=2 * count * units * columns,
            bytes_accessed=2 * units * columns,
            transcendentals=count * units,
        ),
    )(packed, levels, *after)


def route_kernel(owners, ids, gates, table, order, pick, combine, front, copies):
    picks, tokens = ids.shape
    first = pick.shape[1]
    experts = table.shape[1]
    kept = lax.broadcasted_iota(jnp.int32, (owners, experts), 0)
    number = lax.broadcasted_iota(jnp.int32, (owners, experts), 1)
    expert_of = jnp.sum(jnp.where(table[...] == kept, number, 0), axis=1, keepdims=True)
    hit = jnp.zeros((owners, tokens), jnp.float32)
    weight = jnp.zeros((owners, tokens), jnp.float32)
    for k in range(picks):
        match = ids[k : k + 1, :] == expert_of
        hit = jnp.where(match, 1.0, hit)
        weight = jnp.where(match, gates[k : k + 1, :].astype(jnp.float32) / 256.0, weight)
    picked = jnp.max(hit, axis=0, keepdims=True)
    row = lax.broadcasted_iota(jnp.int32, (tokens, tokens), 0)
    column = lax.broadcasted_iota(jnp.int32, (tokens, tokens), 1)
    earlier = (row < column).astype(jnp.float32).astype(jnp.bfloat16)

    def before(flags):
        wide = jnp.broadcast_to(flags, (max(8, flags.shape[0]), tokens)).astype(jnp.bfloat16)
        return jnp.dot(wide, earlier, preferred_element_type=jnp.float32)[: flags.shape[0]]

    ahead = before(picked)
    token = lax.broadcasted_iota(jnp.int32, (1, tokens), 1).astype(jnp.float32)
    count = jnp.sum(picked, axis=1, keepdims=True)
    place = jnp.where(picked > 0.0, ahead, count + token - ahead).astype(jnp.int32)
    moved = (row == place).astype(jnp.float32)
    order[...] = moved.astype(jnp.bfloat16)
    front[...] = moved[:first].astype(jnp.bfloat16)
    for chip in range(copies.shape[0] // first):
        copies[chip * first : (chip + 1) * first, :] = moved[:first].astype(jnp.bfloat16)
    position = before(hit)
    spot = lax.broadcasted_iota(jnp.int32, (CAP, tokens), 0).astype(jnp.float32)
    chosen_rows, weighted = [], []
    for s in range(owners):
        select = jnp.where(position[s : s + 1] == spot, hit[s : s + 1], 0.0)
        chosen_rows.append(select)
        weighted.append(select * weight[s : s + 1])
    combine[...] = jnp.concatenate(weighted, axis=0).astype(jnp.bfloat16)
    pick[...] = lax.dot_general(
        jnp.concatenate(chosen_rows, axis=0).astype(jnp.bfloat16),
        moved[:first].astype(jnp.bfloat16),
        (((1,), (1,)), ((), ())),
        preferred_element_type=jnp.float32,
    ).astype(jnp.bfloat16)


def route(expert_ids, gate_num, slot_table, owners, first):
    tokens = expert_ids.shape[0]
    slots = owners * CAP
    return pl.pallas_call(
        lambda *refs: route_kernel(owners, *refs),
        out_shape=[
            jax.ShapeDtypeStruct((tokens, tokens), jnp.bfloat16),
            jax.ShapeDtypeStruct((slots, first), jnp.bfloat16),
            jax.ShapeDtypeStruct((slots, tokens), jnp.bfloat16),
            jax.ShapeDtypeStruct((first, tokens), jnp.bfloat16),
            jax.ShapeDtypeStruct((owners // 2 * first, tokens), jnp.bfloat16),
        ],
        cost_estimate=pl.CostEstimate(flops=10**7, bytes_accessed=10**5, transcendentals=0),
    )(expert_ids.T, gate_num.T, slot_table[None, :])


NOPE = 128
ROPE = 64
VHEAD = 128
LATENT = 512


def attend(queries, latent, latent_up):
    seq_len, head_count = queries.shape[:2]
    scale = 1.0 / math.sqrt(NOPE + ROPE)
    key_value = jnp.einsum(
        "tc,hcd->thd", latent[:, :LATENT], latent_up, preferred_element_type=jnp.float32
    ).astype(jnp.bfloat16)
    rotary = jnp.broadcast_to(latent[:, None, LATENT:], (seq_len, head_count, ROPE))
    keys = jnp.concatenate([key_value[:, :, :NOPE], rotary], axis=2)
    scores = jnp.einsum("thd,shd->hts", queries, keys, preferred_element_type=jnp.float32) * scale
    causal = jnp.arange(seq_len)[None, :] <= jnp.arange(seq_len)[:, None]
    scores = jnp.where(causal[None], scores, -1e30)
    top = jnp.max(scores, axis=2, keepdims=True)
    expo = jnp.exp(scores - top)
    probs = (expo / jnp.sum(expo, axis=2, keepdims=True)).astype(jnp.bfloat16)
    result = jnp.einsum(
        "hts,shd->thd", probs, key_value[:, :, NOPE:], preferred_element_type=jnp.float32
    )
    return result.astype(jnp.bfloat16).reshape(seq_len, head_count * VHEAD)


def chosen(onehot, rows):
    return jnp.dot(onehot, rows, preferred_element_type=jnp.float32).astype(jnp.bfloat16)


def same_cores(chips):
    return [[2 * chip + core for chip in range(chips)] for core in range(2)]


def across_chips(chunks):
    groups = same_cores(chunks.shape[0])
    return lax.all_to_all(
        chunks, "dp", split_axis=0, concat_axis=0, axis_index_groups=groups, tiled=True
    )


def to_other_chips(chunks):
    owners = 2 * len(chunks)
    moved = [chunks[0]]
    for turn in range(1, len(chunks)):
        pairs = [(place, place ^ (2 * turn)) for place in range(owners)]
        moved.append(lax.ppermute(chunks[turn], "dp", pairs))
    return moved


def in_order_of_ranks(chunks, after):
    ranks = len(chunks)
    chip = lax.div(lax.axis_index("dp"), 2)
    turned = lax.rem(lax.axis_index("tensor") + jnp.arange(ranks, dtype=jnp.int32), ranks)
    return arrange(jnp.bitwise_xor(chip, turned), chunks, after)


def to_other_ranks(chunks):
    ranks = len(chunks)
    moved = [chunks[0]]
    for shift in range(1, ranks):
        pairs = [(place, (place + shift) % ranks) for place in range(ranks)]
        moved.append(lax.ppermute(chunks[shift], "tensor", pairs))
    return moved


def across_ranks(chunks, ranks):
    chips, rows, width = chunks.shape
    chunks = chunks.reshape(ranks, chips // ranks, rows, width)
    return lax.all_to_all(chunks, "tensor", split_axis=0, concat_axis=0, tiled=True)


def shards(
    residual_in,
    queries,
    latent,
    latent_up,
    out_proj,
    norm_gain,
    expert_ids,
    gate_num,
    slot_table,
    gate_proj,
    up_proj,
    down_proj,
    inv_chol,
):
    seq_len, model_cols = residual_in.shape
    owners = lax.axis_size("dp")
    ranks = lax.axis_size("tensor")

    chips = owners // 2
    first = min(seq_len, owners * CAP) if chips == ranks == 4 else seq_len
    core = lax.rem(lax.axis_index("dp"), 2)[None]
    partner = lax.ppermute(out_proj, "dp", [(i, i ^ 1) for i in range(owners)])
    order_rows, pick, combine, order_first, order_copies = route(
        expert_ids, gate_num, slot_table, owners, first
    )
    factors = scaled_factors(inv_chol[0])
    weight = down_proj[0]
    panels = factors.shape[0]
    attended = attend(queries, latent, latent_up)

    copies = chosen(order_copies, attended)
    everyone = across_chips(copies.reshape(chips, first, -1))
    later = []
    if first < seq_len and chips == ranks:
        later = to_other_chips([chosen(order_rows[first:], attended)] * chips)
    partly = [quantize_panel(0, factors[0], weight, [], copies, *later[:1])]
    chunks = project(core, [everyone], out_proj, partner, partly[0])[0]
    arrived = across_chips(chunks)
    for panel in range(1, panels):
        partly = [quantize_panel(panel, factors[panel], weight, partly, chunks)]
    if later:
        later = project(core, later, out_proj, partner, partly[0])
    quantized = partly[0]
    front, outgoing = make_front(
        across_ranks(arrived, ranks), order_first, residual_in, pick, quantized
    )
    incoming = lax.all_to_all(
        outgoing.reshape(owners, CAP, -1), "dp", split_axis=0, concat_axis=0, tiled=True
    )
    packed = gate_and_up(
        incoming.reshape(owners * CAP, -1),
        norm_gain[None, :],
        gate_proj[0],
        up_proj[0],
        ranks,
        *later,
    )
    packed = lax.all_to_all(packed, "tensor", split_axis=0, concat_axis=0, tiled=True)
    if later:
        later = in_order_of_ranks(to_other_chips(later), outgoing)
    expert_part, gram = expert_outputs(packed, quantized, model_cols * ranks, *later)
    if later:
        later = to_other_ranks(later)
    ordered_out = front
    if later:
        ordered_in = chosen(order_rows[first:], residual_in).astype(jnp.float32)
        back = ordered_in + sum(chunk.astype(jnp.float32) for chunk in later)
        ordered_out = jnp.concatenate([front, back.astype(jnp.bfloat16)], axis=0)
    residual_out = lax.dot_general(
        order_rows, ordered_out, (((0,), (0,)), ((), ())), preferred_element_type=jnp.float32
    ).astype(jnp.bfloat16)

    parcels = (
        expert_part.reshape(owners, CAP, ranks, model_cols)
        .swapaxes(1, 2)
        .reshape(owners * ranks, CAP, model_cols)
    )
    returned = lax.all_to_all(
        parcels, ("dp", "tensor"), split_axis=0, concat_axis=0, tiled=True
    ).reshape(owners * ranks * CAP, model_cols)
    weights = jnp.broadcast_to(
        combine.reshape(owners, 1, CAP, seq_len), (owners, ranks, CAP, seq_len)
    ).reshape(owners * ranks * CAP, seq_len)
    moe = lax.dot_general(
        weights, returned, (((0,), (0,)), ((), ())), preferred_element_type=jnp.float32
    )
    return (
        residual_out,
        moe.astype(jnp.bfloat16),
        quantized[None],
        gram[None],
    )


def solution(mesh):
    placed = (
        P("dp", "tensor"),
        P("dp", "tensor", None),
        P("dp", None),
        P("tensor", None, None),
        P("tensor", "dp"),
        P("tensor"),
        P("dp", None),
        P("dp", None),
        P(),
        P("dp", "tensor", None),
        P("dp", "tensor", None),
        P("dp", "tensor", None),
        P("dp", "tensor", None),
    )
    return jax.shard_map(
        shards,
        mesh=mesh,
        in_specs=placed,
        out_specs=(
            P("dp", "tensor"),
            P("dp", "tensor"),
            P("dp", "tensor", None),
            P("dp", "tensor", None),
        ),
        check_vma=False,
    )
```

```python
import math

import jax
import jax.numpy as jnp
import numpy as np
from jax import lax
from jax.experimental import pallas as pl
from jax.experimental.pallas import tpu as pltpu
from jax.sharding import PartitionSpec as P

PANEL = 128
BLK = 16
LANES = 128
SUBS = 8
CAP = 8
ROUNDER = 12582912.0
VMEM_LIMIT = 60 * 2**20


def wave_coefficients():
    nodes = 0.5 * np.cos(np.pi * (np.arange(400) + 0.5) / 800)
    values = nodes - np.sin(2 * np.pi * nodes) / (2 * np.pi)
    basis = np.stack([nodes ** (2 * power + 1) for power in range(6)], axis=1)
    return [float(c) for c in np.linalg.lstsq(basis, values, rcond=None)[0]]


WAVE = wave_coefficients()


def split_bf16(x):
    first = x.astype(jnp.bfloat16)
    rest = x - first.astype(jnp.float32)
    second = rest.astype(jnp.bfloat16)
    third = (rest - second.astype(jnp.float32)).astype(jnp.bfloat16)
    return first, second, third


def quantize_kernel(top, held, scalars, factor, source, *rest):
    done = rest[:held]
    out, weight, nat, rows, errs, levs, levels, lows, steps, scales, in_sem, out_sem, done_sem, back_sem, bounce = rest[-15:]
    columns = nat.shape[1]
    groups = columns // (SUBS * LANES)
    width = groups * SUBS
    blocks = PANEL // BLK

    def fetch(c):
        lanes = pl.ds(c * SUBS * LANES, SUBS * LANES)
        return pltpu.make_async_copy(
            source.at[pl.ds(top, PANEL), lanes], weight.at[:, lanes], in_sem.at[c]
        )

    for c in range(groups):
        fetch(c).start()
    carried = [pltpu.make_async_copy(ref, bounce, done_sem) for ref in done]
    for copy in carried:
        copy.start()
    for c in range(groups):
        fetch(c).wait()
        low, high = [], []
        for s in range(SUBS):
            lanes = pl.ds((c * SUBS + s) * LANES, LANES)
            block = weight[:, lanes].astype(jnp.float32)
            nat[:, lanes] = block
            low.append(jnp.min(block, axis=0, keepdims=True))
            high.append(jnp.max(block, axis=0, keepdims=True))
        low = jnp.concatenate(low, axis=0)
        high = jnp.concatenate(high, axis=0)
        step = (high - low) / 15.0 + 1e-05
        spot = pl.ds(c * SUBS, SUBS)
        lows[spot, :] = low
        steps[spot, :] = step
        scales[spot, :] = 1.0 / step

    for copy in carried:
        copy.wait()
    returned = [pltpu.make_async_copy(bounce, out.at[pl.ds(0, top), :], back_sem) for _ in done]
    for copy in returned:
        copy.start()

    def finish(b):
        spot = b * BLK if isinstance(b, int) else pl.multiple_of(b * BLK, BLK)
        return pltpu.make_async_copy(
            levels.at[pl.ds(spot, BLK), :], out.at[pl.ds(top + spot, BLK), :], out_sem.at[b]
        )

    def block_step(b, first_row):
        base = b * BLK if isinstance(b, int) else pl.multiple_of(b * BLK, BLK)
        for g in range(width):
            rows[pl.ds(g, BLK, stride=width), :] = nat[
                pl.ds(base, BLK), g * LANES : (g + 1) * LANES
            ]
        for k in range(BLK):
            here = pl.ds(k * width, width)
            current = rows[here, :]
            for i in range(k):
                current = current - scalars[base + i, base + k] * errs[pl.ds(i * width, width), :]
            low = lows[...]
            t = jnp.clip((current - low) * scales[...], 0.0, 15.0)
            whole = (t + ROUNDER) - ROUNDER
            u = t - whole
            square = u * u
            fourth = square * square
            wave = (WAVE[0] + WAVE[1] * square) + fourth * (
                (WAVE[2] + WAVE[3] * square) + fourth * (WAVE[4] + WAVE[5] * square)
            )
            level = low + steps[...] * (whole + wave * u)
            errs[here, :] = current - level
            levs[here, :] = level
        column = lax.broadcasted_iota(jnp.int32, (BLK, PANEL), 1)
        coupling = jnp.where(column >= base + BLK, factor[pl.ds(base, BLK), :], 0.0)
        u1, u2, u3 = split_bf16(coupling)
        left = jnp.concatenate([u1, u1, u1, u2, u2, u3], axis=0)[:, first_row:]
        for c in range(groups):

            def natural(ref):
                pieces = [
                    ref[pl.ds(c * SUBS + s, BLK, stride=width), :] for s in range(SUBS)
                ]
                return jnp.concatenate(pieces, axis=1)

            span = slice(c * SUBS * LANES, (c + 1) * SUBS * LANES)
            levels[pl.ds(base, BLK), span] = natural(levs).astype(levels.dtype)
            if first_row == PANEL:
                continue
            e1, e2, e3 = split_bf16(natural(errs))
            right = jnp.concatenate([e1, e2, e3, e1, e2, e1], axis=0)
            update = lax.dot_general(
                left, right, (((0,), (0,)), ((), ())), preferred_element_type=jnp.float32
            )
            nat[first_row:, span] = nat[first_row:, span] - update
        finish(b).start()

    for begin in range(0, blocks - 2, 2):

        def body(b, carry):
            block_step(b, (begin + 1) * BLK)
            return carry

        lax.fori_loop(begin, begin + 2, body, 0)
    block_step(blocks - 2, (blocks - 1) * BLK)
    block_step(blocks - 1, PANEL)
    for b in range(blocks):
        finish(b).wait()
    for copy in returned:
        copy.wait()


def quantize_panel(index, factor, weight, partly, *after):
    columns = weight.shape[1]
    width = columns // LANES
    wide = pltpu.VMEM((BLK * width, LANES), jnp.float32)
    small = pltpu.VMEM((width, LANES), jnp.float32)
    anywhere = pl.BlockSpec(memory_space=pl.ANY)
    return pl.pallas_call(
        lambda *refs: quantize_kernel(index * PANEL, len(partly), *refs),
        out_shape=jax.ShapeDtypeStruct(((index + 1) * PANEL, columns), jnp.bfloat16),
        in_specs=[
            pl.BlockSpec(memory_space=pltpu.SMEM),
            pl.BlockSpec(memory_space=pltpu.VMEM),
            anywhere,
        ]
        + [anywhere] * (len(partly) + len(after)),
        out_specs=anywhere,
        scratch_shapes=[
            pltpu.VMEM((PANEL, columns), jnp.bfloat16),
            pltpu.VMEM((PANEL, columns), jnp.float32),
            wide,
            wide,
            wide,
            pltpu.VMEM((PANEL, columns), jnp.bfloat16),
            small,
            small,
            small,
            pltpu.SemaphoreType.DMA((columns // (SUBS * LANES),)),
            pltpu.SemaphoreType.DMA((PANEL // BLK,)),
            pltpu.SemaphoreType.DMA,
            pltpu.SemaphoreType.DMA,
            pltpu.VMEM((max(1, index) * PANEL, columns), jnp.bfloat16),
        ],
        compiler_params=pltpu.CompilerParams(vmem_limit_bytes=VMEM_LIMIT),
        cost_estimate=pl.CostEstimate(
            flops=16 * 10**9, bytes_accessed=4 * PANEL * columns, transcendentals=0
        ),
    )(factor, factor, weight, *partly, *after)


def scaled_factors(upper):
    blocks = upper.reshape(-1, PANEL, PANEL)
    index = jnp.arange(PANEL)
    diagonal = jnp.sum(
        jnp.where(index[:, None] == index[None, :], blocks, 0.0), axis=2, keepdims=True
    )
    return jnp.where(index[:, None] < index[None, :], blocks / diagonal, 0.0)


def project_kernel(arrays, core, own, partner, *rest):
    rows = rest[:arrays]
    outs = rest[-arrays - 6 : -6]
    columns, left, low, high, column_sem, row_sem = rest[-6:]
    tiles = column_sem.shape[1]
    tile = columns.shape[1] // tiles
    copies = []
    for k in range(tiles):
        span = pl.ds(k * tile, tile)
        for source, turn in ((own, core[0]), (partner, 1 - core[0])):
            copies.append(
                pltpu.make_async_copy(
                    source.at[span, :],
                    columns.at[turn, span, :],
                    column_sem.at[len(copies) % 2, k],
                )
            )
    joined = len(rows[0].shape) == 3
    gathers = [
        pltpu.make_async_copy(ref, left if joined else left.at[g], row_sem.at[g])
        for g, ref in enumerate(rows)
    ]
    for copy in gathers + copies:
        copy.start()
    for copy in gathers:
        copy.wait()
    for k in range(tiles):
        copies[2 * k].wait()
        copies[2 * k + 1].wait()
        span = slice(k * tile, (k + 1) * tile)
        part = left[:, :, span].reshape(-1, tile)
        for half, total in enumerate((low, high)):
            product = jnp.dot(part, columns[half, span, :], preferred_element_type=jnp.float32)
            total[...] = product if k == 0 else total[...] + product
    count = left.shape[1]
    width = own.shape[1]
    for g in range(left.shape[0]):
        out = outs[0].at[g] if joined else outs[g]
        span = slice(g * count, (g + 1) * count)
        out[:, :width] = low[span, :].astype(jnp.bfloat16)
        out[:, width:] = high[span, :].astype(jnp.bfloat16)


def project(core, rows, own, partner, *after):
    joined = rows[0].ndim == 3
    groups = rows[0].shape[0] if joined else len(rows)
    count, depth = rows[0].shape[-2:]
    width = own.shape[1]
    shape = (groups,) * joined + (count, 2 * width)
    tiles = depth // 512
    total = groups * count
    vmem = pl.BlockSpec(memory_space=pltpu.VMEM)
    anywhere = pl.BlockSpec(memory_space=pl.ANY)
    return pl.pallas_call(
        lambda *refs: project_kernel(len(rows), *refs),
        out_shape=[jax.ShapeDtypeStruct(shape, jnp.bfloat16)] * len(rows),
        in_specs=[pl.BlockSpec(memory_space=pltpu.SMEM)]
        + [anywhere] * (2 + len(rows) + len(after)),
        out_specs=[vmem] * len(rows),
        scratch_shapes=[
            pltpu.VMEM((2, depth, width), jnp.bfloat16),
            pltpu.VMEM((groups, count, depth), jnp.bfloat16),
            pltpu.VMEM((total, width), jnp.float32),
            pltpu.VMEM((total, width), jnp.float32),
            pltpu.SemaphoreType.DMA((2, tiles)),
            pltpu.SemaphoreType.DMA((groups,)),
        ],
        compiler_params=pltpu.CompilerParams(vmem_limit_bytes=VMEM_LIMIT),
        cost_estimate=pl.CostEstimate(
            flops=4 * total * depth * width,
            bytes_accessed=2 * (total * depth + 2 * depth * width + 2 * total * width),
            transcendentals=0,
        ),
    )(core, own, partner, *rows, *after)


def front_kernel(arrived, order, residual, pick, *rest):
    front, outgoing = rest[-2:]
    ranks, per, _, width = arrived.shape
    base = jnp.dot(order[...], residual[...], preferred_element_type=jnp.float32)
    for block in range(per):
        span = slice(block * width, (block + 1) * width)
        total = sum(arrived[rank, block].astype(jnp.float32) for rank in range(ranks))
        front[:, span] = (base[:, span] + total).astype(front.dtype)
    outgoing[...] = jnp.dot(
        pick[...], front[...], preferred_element_type=jnp.float32
    ).astype(outgoing.dtype)


def make_front(arrived, order, residual, pick, *after):
    columns = residual.shape[1]
    vmem = pl.BlockSpec(memory_space=pltpu.VMEM)
    return pl.pallas_call(
        front_kernel,
        out_shape=[
            jax.ShapeDtypeStruct((order.shape[0], columns), jnp.bfloat16),
            jax.ShapeDtypeStruct((pick.shape[0], columns), jnp.bfloat16),
        ],
        in_specs=[vmem] * 4 + [pl.BlockSpec(memory_space=pl.ANY)] * len(after),
        out_specs=[vmem, vmem],
        compiler_params=pltpu.CompilerParams(vmem_limit_bytes=VMEM_LIMIT),
        cost_estimate=pl.CostEstimate(
            flops=10**8, bytes_accessed=2 * arrived.size, transcendentals=0
        ),
    )(arrived, order, residual, pick, *after)


def arrange_kernel(count, spots, *rest):
    chunks, outs = rest[:count], rest[-count:]
    for place, out in enumerate(outs):
        for number, chunk in enumerate(chunks):

            @pl.when(spots[place] == number)
            def _():
                out[...] = chunk[...]


def arrange(spots, chunks, *after):
    vmem = pl.BlockSpec(memory_space=pltpu.VMEM)
    return pl.pallas_call(
        lambda *refs: arrange_kernel(len(chunks), *refs),
        out_shape=[jax.ShapeDtypeStruct(chunk.shape, chunk.dtype) for chunk in chunks],
        in_specs=[pl.BlockSpec(memory_space=pltpu.SMEM)]
        + [vmem] * len(chunks)
        + [pl.BlockSpec(memory_space=pl.ANY)] * len(after),
        out_specs=[vmem] * len(chunks),
        compiler_params=pltpu.CompilerParams(vmem_limit_bytes=VMEM_LIMIT),
        cost_estimate=pl.CostEstimate(
            flops=0, bytes_accessed=4 * len(chunks) * chunks[0].size, transcendentals=0
        ),
    )(spots, *chunks, *after)


def gate_kernel(rows, gain, gate_w, up_w, *rest):
    packed, weights, gate, up, scaled, sem = rest[-6:]
    tiles = sem.shape[1]
    tile = weights.shape[1] // tiles
    copies = []
    for k in range(tiles):
        span = pl.ds(k * tile, tile)
        for which, source in enumerate((gate_w, up_w)):
            copies.append(
                pltpu.make_async_copy(
                    source.at[span, :], weights.at[which, span, :], sem.at[which, k]
                )
            )
    for copy in copies:
        copy.start()
    wide = rows[...].astype(jnp.float32)
    squares = jnp.sum(wide * wide, axis=1, keepdims=True)
    scaled[...] = (wide * gain[...].astype(jnp.float32)).astype(jnp.bfloat16)
    for k in range(tiles):
        span = slice(k * tile, (k + 1) * tile)
        for which, total in enumerate((gate, up)):
            copies[2 * k + which].wait()
            product = jnp.dot(
                scaled[:, span], weights[which, span, :], preferred_element_type=jnp.float32
            )
            total[...] = product if k == 0 else total[...] + product
    high = squares.astype(jnp.bfloat16).astype(jnp.float32)
    lane = lax.broadcasted_iota(jnp.int32, (rows.shape[0], LANES), 1)
    tail = jnp.where(lane == 0, high, jnp.where(lane == 1, squares - high, 0.0))
    ranks, _, width = packed.shape
    units = (width - LANES) // 2
    for rank in range(ranks):
        span = slice(rank * units, (rank + 1) * units)
        packed[rank, :, :units] = gate[:, span].astype(packed.dtype)
        packed[rank, :, units : 2 * units] = up[:, span].astype(packed.dtype)
        packed[rank, :, 2 * units :] = tail.astype(packed.dtype)


def gate_and_up(rows, gain, gate_w, up_w, ranks, *after):
    count, columns = rows.shape
    hidden = gate_w.shape[1]
    tiles = 7
    shape = (ranks, count, 2 * hidden // ranks + LANES)
    vmem = pl.BlockSpec(memory_space=pltpu.VMEM)
    anywhere = pl.BlockSpec(memory_space=pl.ANY)
    return pl.pallas_call(
        gate_kernel,
        out_shape=jax.ShapeDtypeStruct(shape, jnp.bfloat16),
        in_specs=[vmem, vmem, anywhere, anywhere] + [anywhere] * len(after),
        out_specs=vmem,
        scratch_shapes=[
            pltpu.VMEM((2, columns, hidden), jnp.bfloat16),
            pltpu.VMEM((count, hidden), jnp.float32),
            pltpu.VMEM((count, hidden), jnp.float32),
            pltpu.VMEM((count, columns), jnp.bfloat16),
            pltpu.SemaphoreType.DMA((2, tiles)),
        ],
        compiler_params=pltpu.CompilerParams(vmem_limit_bytes=VMEM_LIMIT),
        cost_estimate=pl.CostEstimate(
            flops=4 * count * columns * hidden,
            bytes_accessed=4 * columns * hidden,
            transcendentals=0,
        ),
    )(rows, gain, gate_w, up_w, *after)


def expert_kernel(model_width, packed, levels, *rest):
    out, gram, held, sem = rest[-4:]
    ranks, count, width = packed.shape
    units = (width - LANES) // 2
    tiles = sem.shape[0]
    tile = held.shape[1] // tiles
    copies = []
    for k in range(tiles):
        span = pl.ds(k * tile, tile)
        copies.append(pltpu.make_async_copy(levels.at[:, span], held.at[:, span], sem.at[k]))
    for copy in copies:
        copy.start()
    summed = sum(packed[rank].astype(jnp.float32) for rank in range(ranks))
    tail = summed[:, 2 * units :]
    lane = lax.broadcasted_iota(jnp.int32, tail.shape, 1)
    squares = jnp.sum(jnp.where(lane < 2, tail, 0.0), axis=1, keepdims=True)
    inverse = lax.rsqrt(squares / model_width + 1e-06)
    gate = summed[:, :units] * inverse
    up = summed[:, units : 2 * units] * inverse
    active = (gate / (1.0 + jnp.exp(-gate)) * up).astype(jnp.bfloat16)
    for panel in range(units // PANEL):
        span = slice(panel * PANEL, (panel + 1) * PANEL)
        gram[span, :] = (
            lax.dot_general(
                active[:, span],
                active[:, span],
                (((0,), (0,)), ((), ())),
                preferred_element_type=jnp.float32,
            )
            / count
        )
    for k in range(tiles):
        span = slice(k * tile, (k + 1) * tile)
        copies[k].wait()
        out[:, span] = jnp.dot(
            active, held[:, span], preferred_element_type=jnp.float32
        ).astype(out.dtype)


def expert_outputs(packed, levels, model_width, *after):
    ranks, count, width = packed.shape
    units, columns = levels.shape
    vmem = pl.BlockSpec(memory_space=pltpu.VMEM)
    anywhere = pl.BlockSpec(memory_space=pl.ANY)
    return pl.pallas_call(
        lambda *refs: expert_kernel(model_width, *refs),
        out_shape=[
            jax.ShapeDtypeStruct((count, columns), jnp.bfloat16),
            jax.ShapeDtypeStruct((units, PANEL), jnp.float32),
        ],
        in_specs=[vmem, anywhere] + [anywhere] * len(after),
        out_specs=[vmem, vmem],
        scratch_shapes=[
            pltpu.VMEM((units, columns), jnp.bfloat16),
            pltpu.SemaphoreType.DMA((7,)),
        ],
        compiler_params=pltpu.CompilerParams(vmem_limit_bytes=VMEM_LIMIT),
        cost_estimate=pl.CostEstimate(
            flops=2 * count * units * columns,
            bytes_accessed=2 * units * columns,
            transcendentals=count * units,
        ),
    )(packed, levels, *after)


def route_kernel(owners, ids, gates, table, order, pick, combine, front, copies):
    picks, tokens = ids.shape
    first = pick.shape[1]
    experts = table.shape[1]
    kept = lax.broadcasted_iota(jnp.int32, (owners, experts), 0)
    number = lax.broadcasted_iota(jnp.int32, (owners, experts), 1)
    expert_of = jnp.sum(jnp.where(table[...] == kept, number, 0), axis=1, keepdims=True)
    hit = jnp.zeros((owners, tokens), jnp.float32)
    weight = jnp.zeros((owners, tokens), jnp.float32)
    for k in range(picks):
        match = ids[k : k + 1, :] == expert_of
        hit = jnp.where(match, 1.0, hit)
        weight = jnp.where(match, gates[k : k + 1, :].astype(jnp.float32) / 256.0, weight)
    picked = jnp.max(hit, axis=0, keepdims=True)
    row = lax.broadcasted_iota(jnp.int32, (tokens, tokens), 0)
    column = lax.broadcasted_iota(jnp.int32, (tokens, tokens), 1)
    earlier = (row < column).astype(jnp.float32).astype(jnp.bfloat16)

    def before(flags):
        wide = jnp.broadcast_to(flags, (max(8, flags.shape[0]), tokens)).astype(jnp.bfloat16)
        return jnp.dot(wide, earlier, preferred_element_type=jnp.float32)[: flags.shape[0]]

    ahead = before(picked)
    token = lax.broadcasted_iota(jnp.int32, (1, tokens), 1).astype(jnp.float32)
    count = jnp.sum(picked, axis=1, keepdims=True)
    place = jnp.where(picked > 0.0, ahead, count + token - ahead).astype(jnp.int32)
    moved = (row == place).astype(jnp.float32)
    order[...] = moved.astype(jnp.bfloat16)
    front[...] = moved[:first].astype(jnp.bfloat16)
    for chip in range(copies.shape[0] // first):
        copies[chip * first : (chip + 1) * first, :] = moved[:first].astype(jnp.bfloat16)
    position = before(hit)
    spot = lax.broadcasted_iota(jnp.int32, (CAP, tokens), 0).astype(jnp.float32)
    chosen_rows, weighted = [], []
    for s in range(owners):
        select = jnp.where(position[s : s + 1] == spot, hit[s : s + 1], 0.0)
        chosen_rows.append(select)
        weighted.append(select * weight[s : s + 1])
    combine[...] = jnp.concatenate(weighted, axis=0).astype(jnp.bfloat16)
    pick[...] = lax.dot_general(
        jnp.concatenate(chosen_rows, axis=0).astype(jnp.bfloat16),
        moved[:first].astype(jnp.bfloat16),
        (((1,), (1,)), ((), ())),
        preferred_element_type=jnp.float32,
    ).astype(jnp.bfloat16)


def route(expert_ids, gate_num, slot_table, owners, first):
    tokens = expert_ids.shape[0]
    slots = owners * CAP
    return pl.pallas_call(
        lambda *refs: route_kernel(owners, *refs),
        out_shape=[
            jax.ShapeDtypeStruct((tokens, tokens), jnp.bfloat16),
            jax.ShapeDtypeStruct((slots, first), jnp.bfloat16),
            jax.ShapeDtypeStruct((slots, tokens), jnp.bfloat16),
            jax.ShapeDtypeStruct((first, tokens), jnp.bfloat16),
            jax.ShapeDtypeStruct((owners // 2 * first, tokens), jnp.bfloat16),
        ],
        cost_estimate=pl.CostEstimate(flops=10**7, bytes_accessed=10**5, transcendentals=0),
    )(expert_ids.T, gate_num.T, slot_table[None, :])


NOPE = 128
ROPE = 64
VHEAD = 128
LATENT = 512


def attend(queries, latent, latent_up):
    seq_len, head_count = queries.shape[:2]
    scale = 1.0 / math.sqrt(NOPE + ROPE)
    key_value = jnp.einsum(
        "tc,hcd->thd", latent[:, :LATENT], latent_up, preferred_element_type=jnp.float32
    ).astype(jnp.bfloat16)
    rotary = jnp.broadcast_to(latent[:, None, LATENT:], (seq_len, head_count, ROPE))
    keys = jnp.concatenate([key_value[:, :, :NOPE], rotary], axis=2)
    scores = jnp.einsum("thd,shd->hts", queries, keys, preferred_element_type=jnp.float32) * scale
    causal = jnp.arange(seq_len)[None, :] <= jnp.arange(seq_len)[:, None]
    scores = jnp.where(causal[None], scores, -1e30)
    top = jnp.max(scores, axis=2, keepdims=True)
    expo = jnp.exp(scores - top)
    probs = (expo / jnp.sum(expo, axis=2, keepdims=True)).astype(jnp.bfloat16)
    result = jnp.einsum(
        "hts,shd->thd", probs, key_value[:, :, NOPE:], preferred_element_type=jnp.float32
    )
    return result.astype(jnp.bfloat16).reshape(seq_len, head_count * VHEAD)


def chosen(onehot, rows):
    return jnp.dot(onehot, rows, preferred_element_type=jnp.float32).astype(jnp.bfloat16)


def same_cores(chips):
    return [[2 * chip + core for chip in range(chips)] for core in range(2)]


def across_chips(chunks):
    groups = same_cores(chunks.shape[0])
    return lax.all_to_all(
        chunks, "dp", split_axis=0, concat_axis=0, axis_index_groups=groups, tiled=True
    )


def to_other_chips(chunks):
    owners = 2 * len(chunks)
    moved = [chunks[0]]
    for turn in range(1, len(chunks)):
        pairs = [(place, place ^ (2 * turn)) for place in range(owners)]
        moved.append(lax.ppermute(chunks[turn], "dp", pairs))
    return moved


def in_order_of_ranks(chunks, after):
    ranks = len(chunks)
    chip = lax.div(lax.axis_index("dp"), 2)
    turned = lax.rem(lax.axis_index("tensor") + jnp.arange(ranks, dtype=jnp.int32), ranks)
    return arrange(jnp.bitwise_xor(chip, turned), chunks, after)


def to_other_ranks(chunks):
    ranks = len(chunks)
    moved = [chunks[0]]
    for shift in range(1, ranks):
        pairs = [(place, (place + shift) % ranks) for place in range(ranks)]
        moved.append(lax.ppermute(chunks[shift], "tensor", pairs))
    return moved


def across_ranks(chunks, ranks):
    chips, rows, width = chunks.shape
    chunks = chunks.reshape(ranks, chips // ranks, rows, width)
    return lax.all_to_all(chunks, "tensor", split_axis=0, concat_axis=0, tiled=True)


def shards(
    residual_in,
    queries,
    latent,
    latent_up,
    out_proj,
    norm_gain,
    expert_ids,
    gate_num,
    slot_table,
    gate_proj,
    up_proj,
    down_proj,
    inv_chol,
):
    seq_len, model_cols = residual_in.shape
    owners = lax.axis_size("dp")
    ranks = lax.axis_size("tensor")

    chips = owners // 2
    first = min(seq_len, owners * CAP) if chips == ranks == 4 else seq_len
    core = lax.rem(lax.axis_index("dp"), 2)[None]
    partner = lax.ppermute(out_proj, "dp", [(i, i ^ 1) for i in range(owners)])
    order_rows, pick, combine, order_first, order_copies = route(
        expert_ids, gate_num, slot_table, owners, first
    )
    factors = scaled_factors(inv_chol[0])
    weight = down_proj[0]
    panels = factors.shape[0]
    attended = attend(queries, latent, latent_up)

    copies = chosen(order_copies, attended)
    everyone = across_chips(copies.reshape(chips, first, -1))
    later = []
    if first < seq_len and chips == ranks:
        later = to_other_chips([chosen(order_rows[first:], attended)] * chips)
    partly = [quantize_panel(0, factors[0], weight, [], copies, *later[:1])]
    chunks = project(core, [everyone], out_proj, partner, partly[0])[0]
    arrived = across_chips(chunks)
    for panel in range(1, panels):
        partly = [quantize_panel(panel, factors[panel], weight, partly, chunks)]
    if later:
        later = project(core, later, out_proj, partner, partly[0])
    quantized = partly[0]
    front, outgoing = make_front(
        across_ranks(arrived, ranks), order_first, residual_in, pick, quantized, *later
    )
    incoming = lax.all_to_all(
        outgoing.reshape(owners, CAP, -1), "dp", split_axis=0, concat_axis=0, tiled=True
    )
    if later:
        later = in_order_of_ranks(to_other_chips(later), outgoing)
    packed = gate_and_up(
        incoming.reshape(owners * CAP, -1),
        norm_gain[None, :],
        gate_proj[0],
        up_proj[0],
        ranks,
        *later,
    )
    packed = lax.all_to_all(packed, "tensor", split_axis=0, concat_axis=0, tiled=True)
    expert_part, gram = expert_outputs(packed, quantized, model_cols * ranks)
    if later:
        later = to_other_ranks(later)
    ordered_out = front
    if later:
        ordered_in = chosen(order_rows[first:], residual_in).astype(jnp.float32)
        back = ordered_in + sum(chunk.astype(jnp.float32) for chunk in later)
        ordered_out = jnp.concatenate([front, back.astype(jnp.bfloat16)], axis=0)
    residual_out = lax.dot_general(
        order_rows, ordered_out, (((0,), (0,)), ((), ())), preferred_element_type=jnp.float32
    ).astype(jnp.bfloat16)

    parcels = (
        expert_part.reshape(owners, CAP, ranks, model_cols)
        .swapaxes(1, 2)
        .reshape(owners * ranks, CAP, model_cols)
    )
    returned = lax.all_to_all(
        parcels, ("dp", "tensor"), split_axis=0, concat_axis=0, tiled=True
    ).reshape(owners * ranks * CAP, model_cols)
    weights = jnp.broadcast_to(
        combine.reshape(owners, 1, CAP, seq_len), (owners, ranks, CAP, seq_len)
    ).reshape(owners * ranks * CAP, seq_len)
    moe = lax.dot_general(
        weights, returned, (((0,), (0,)), ((), ())), preferred_element_type=jnp.float32
    )
    return (
        residual_out,
        moe.astype(jnp.bfloat16),
        quantized[None],
        gram[None],
    )


def solution(mesh):
    placed = (
        P("dp", "tensor"),
        P("dp", "tensor", None),
        P("dp", None),
        P("tensor", None, None),
        P("tensor", "dp"),
        P("tensor"),
        P("dp", None),
        P("dp", None),
        P(),
        P("dp", "tensor", None),
        P("dp", "tensor", None),
        P("dp", "tensor", None),
        P("dp", "tensor", None),
    )
    return jax.shard_map(
        shards,
        mesh=mesh,
        in_specs=placed,
        out_specs=(
            P("dp", "tensor"),
            P("dp", "tensor"),
            P("dp", "tensor", None),
            P("dp", "tensor", None),
        ),
        check_vma=False,
    )
```
